32 devices in a mesh: shard: 16 (over z, y, x), rep: 2 (over core).
Axes of the slice: x: 2, y: 2, z: 4, core: 2. Of those that a mesh axis runs over, the one named last changes fastest.
Arguments:
- queries: bfloat16 [128, 32, 128], P(('rep', 'shard')), parts along dimension 0, may hold values from -0.5 to 0.5
- centroids: bfloat16 [32768, 128], P('shard'), may hold values from -0.5 to 0.5
- codes: int32 [512, 128], P('shard'), may hold values from 0 to 2047
- residual_codes: int32 [512, 128, 128], P('shard'), may hold values from 0 to 3
- lengths: int32 [512], P('shard'), may hold values from 1 to 128
- bucket_weights: float32 [4], replicated, may hold values from -0.12 to 0.12
- candidates: int32 [128, 32], P(('rep', 'shard')), parts along dimension 0, may hold values from 0 to 511, as said below
Outputs:
- exact_scores: float32 [128, 32], P(('rep', 'shard')), parts along dimension 0
- approx_scores: float32 [128, 32], P(('rep', 'shard')), parts along dimension 0
The draws below stay inside these ranges and needn't reach their ends.
There are 2 independent parts, one for each index of `rep`. The reference program is written for one: setup_inputs(seed, part) draws one part's arguments, and reference() takes and returns one part's arrays. A program takes and returns all parts, laid end to end along the dimension named above; an argument that names none is the same for every part. Nothing has to cross between parts.
Inputs may be any that keep to these rules, and one draw needn't show every extreme that they name: `candidates`: of the 128 candidate slots of one shard's queries, at most 16 name passages of any one index shard, and some index shard is named by exactly 16 of them.
All inputs are finite; a program needn't handle non-finite values.
Results may differ from the reference program's by a relative error of at most 0.0003.
Values may be sent and summed in bfloat16 or wider, within the bound.
No kernel may reach another device: no remote copies, remote signals or barrier semaphores. Data moves between devices by JAX's collectives and lax.ppermute only.
A program may use at most 128 MiB of HBM per device.

```python
import jax
import jax.numpy as jnp
from jax import lax

D = 128
QT = 32
L = 128
C_DEV = 2048
P_DEV = 32
Q_DEV = 4
K = 32
CAP = 16
QUERIES = 64
PASSAGES = 512
CENT = 32768
N_SHARD = 16


def draw_candidates(key, part):
    hot_key, rest_key = jax.random.split(jax.random.fold_in(key, 17))
    hottest = jax.random.randint(hot_key, (), 0, N_SHARD)
    slot_count = Q_DEV * K
    slot_rank = jnp.arange(slot_count)

    def one_block(block_index):
        block_key = jax.random.fold_in(rest_key, block_index)
        turn_key, perm_key, local_key = jax.random.split(block_key, 3)
        offset = jax.random.randint(turn_key, (), 0, N_SHARD - 1)
        others = (hottest + 1 + (slot_rank - CAP + offset) % (N_SHARD - 1)) % N_SHARD
        target = jnp.where(slot_rank < CAP, hottest, others)
        target = jax.random.permutation(perm_key, target)
        local_id = jax.random.randint(local_key, (slot_count,), 0, P_DEV)
        return (target * P_DEV + local_id).reshape(Q_DEV, K)
    blocks = jax.vmap(one_block)(jnp.arange(N_SHARD))
    return blocks.reshape(Q_DEV * N_SHARD, K).astype(jnp.int32)


def touch_ends(entries, own_key, low, top_value):
    spot = [jax.random.randint(jax.random.fold_in(own_key, axis), (), 0, length) for axis, length in enumerate(entries.shape)]
    longest = entries.shape.index(max(entries.shape))
    neighbour = spot[:longest] + [(spot[longest] + 1) % entries.shape[longest]] + spot[longest + 1:]
    return entries.at[tuple(spot)].set(low).at[tuple(neighbour)].set(top_value)


def shard_levels(key, dims, cuts, least, high):
    def one(axis_at, blocks):
        draws = jax.random.uniform(jax.random.fold_in(jax.random.fold_in(key, 6), axis_at), (blocks,), jnp.float32, least / len(cuts), high / len(cuts))
        return jnp.repeat(jnp.exp(draws), dims[axis_at] // blocks).reshape((-1,) + (1,) * (len(dims) - axis_at - 1))

    factor_of = one(*cuts[0])
    for cut in cuts[1:]:
        factor_of = factor_of * one(*cut)
    return factor_of


def noise(own_key, shape, spread, limit, pieces=(), kind=jnp.bfloat16):
    factor_of = shard_levels(own_key, shape, pieces, -0.22, 0.18) if pieces else 1.0
    array = jax.random.normal(own_key, shape, jnp.float32) * spread * factor_of
    return jnp.minimum(jnp.maximum(array, -limit), limit).astype(kind)


def setup_inputs(seed: int = 0, part: int = 0) -> dict:
    key_list = jax.random.split(jax.random.key(seed), 8)
    own_keys = jax.random.split(jax.random.fold_in(key_list[7], part), 8)
    return {
        "queries": noise(own_keys[0], (QUERIES, QT, D), 0.088, 0.5, ((0, 16),)),
        "centroids": noise(key_list[1], (CENT, D), 0.088, 0.5, ((0, 16),)),
        "codes": touch_ends(jax.random.randint(key_list[2], (PASSAGES, L), 0, C_DEV), jax.random.fold_in(key_list[2], 1), 0, C_DEV - 1).astype(jnp.int32),
        "residual_codes": touch_ends(jax.random.randint(key_list[3], (PASSAGES, L, D), 0, 4), jax.random.fold_in(key_list[3], 1), 0, 3).astype(jnp.int32),
        "lengths": touch_ends(jax.random.randint(key_list[4], (PASSAGES,), 1, L + 1), jax.random.fold_in(key_list[4], 1), 1, L).astype(jnp.int32),
        "bucket_weights": jnp.clip(jax.random.uniform(key_list[5], (4,), jnp.float32, -0.12, 0.12), -0.12, 0.12),
        "candidates": draw_candidates(jax.random.fold_in(jax.random.fold_in(key_list[7], part), 71), part),
    }


def decompress(centroid_rows, residual_codes, bucket_weights):
    levels = jnp.zeros(residual_codes.shape, jnp.float32)
    for bucket_index in range(4):
        levels = levels + jnp.where(residual_codes == bucket_index, bucket_weights[bucket_index], 0.0)
    values = centroid_rows.astype(jnp.float32) + levels
    return (values * lax.rsqrt(lax.optimization_barrier(jnp.sum(values * values, axis=-1, keepdims=True)) + 1e-06)).astype(jnp.bfloat16)

def max_sum(dots, live_tokens):
    masked = jnp.where(live_tokens[:, None, :], dots, -jnp.inf)
    return lax.optimization_barrier(jnp.sum(lax.optimization_barrier(jnp.max(masked, axis=-1)), axis=-1))

def reference(queries, centroids, codes, residual_codes, lengths, bucket_weights, candidates):

    def one_query(inputs):
        query_rows, cand_ids = inputs
        owner_shard = (cand_ids // P_DEV).astype(jnp.int32)
        token_codes = codes[cand_ids]
        cent_rows = centroids[owner_shard[:, None] * C_DEV + token_codes]
        passage_rows = decompress(cent_rows, residual_codes[cand_ids], bucket_weights)
        live_tokens = jnp.arange(L)[None, :] < lengths[cand_ids][:, None]
        query_wide = query_rows.astype(jnp.float32)
        approx = max_sum(jnp.einsum('td,kjd->ktj', query_wide, cent_rows.astype(jnp.float32)), live_tokens)
        exact = max_sum(jnp.einsum('td,kjd->ktj', query_wide, passage_rows.astype(jnp.float32)), live_tokens)
        return (exact, approx)
    exact_scores, approx_scores = lax.map(one_query, (queries, candidates))
    return (exact_scores, approx_scores)
```

```python
import functools

import jax
import jax.numpy as jnp
from jax import lax
from jax.experimental import pallas as pl
from jax.experimental.pallas import tpu as pltpu
from jax.sharding import PartitionSpec as P

GROUP = 256
STEP = 4
CHUNK = 256
TILE = 4


def decompress_kernel(lengths, weights, codes, residuals, centroids, rows_out, table):
    step = pl.program_id(0)
    passages, slots = codes.shape
    groups = centroids.shape[0] // GROUP
    width = centroids.shape[1]

    @pl.when(step == 0)
    def _():
        for g in range(groups):
            table[:, g * width : (g + 1) * width] = centroids[g * GROUP : (g + 1) * GROUP, :]

    code_rows = codes[...].astype(jnp.float32)
    code_cols = jnp.swapaxes(code_rows, 0, 1).astype(jnp.int32)
    lane = lax.broadcasted_iota(jnp.int32, (slots, GROUP), 1)
    token = lax.broadcasted_iota(jnp.int32, (slots, width), 0)
    hot = []
    high = []
    for p in range(passages):
        code = code_cols[:, p : p + 1]
        hot.append((lane == (code % GROUP)).astype(jnp.bfloat16))
        high.append(jnp.broadcast_to(code // GROUP, (slots, width)))
    spread = jnp.dot(
        jnp.concatenate(hot, 0), table[...], preferred_element_type=jnp.float32
    )
    for p in range(passages):
        part = spread[p * slots : (p + 1) * slots]
        cent = part[:, :width]
        for g in range(1, groups):
            cent = jnp.where(high[p] == g, part[:, g * width : (g + 1) * width], cent)
        code = residuals[p]
        odd = (code & 1) == 1
        low = jnp.where(odd, weights[1], weights[0])
        top = jnp.where(odd, weights[3], weights[2])
        values = cent + jnp.where(code >= 2, top, low)
        norm = lax.rsqrt(jnp.sum(values * values, axis=-1, keepdims=True) + 1e-06)
        exact = values * norm
        live = token < lengths[step * passages + p]
        exact = jnp.where(live, exact, exact[0:1, :])
        cent = jnp.where(live, cent, cent[0:1, :])
        rows_out[p, :slots, :] = exact.astype(jnp.bfloat16)
        rows_out[p, slots:, :] = cent.astype(jnp.bfloat16)


def decompress(centroids, codes, residual_codes, lengths, bucket_weights):
    passages, slots = codes.shape
    count, width = centroids.shape
    return pl.pallas_call(
        decompress_kernel,
        grid=(passages // STEP,),
        in_specs=[
            pl.BlockSpec(memory_space=pltpu.SMEM),
            pl.BlockSpec(memory_space=pltpu.SMEM),
            pl.BlockSpec((None, STEP, slots), lambda i: (i, 0, 0)),
            pl.BlockSpec((STEP, slots, width), lambda i: (i, 0, 0)),
            pl.BlockSpec((count, width), lambda i: (0, 0)),
        ],
        out_specs=pl.BlockSpec((STEP, 2 * slots, width), lambda i: (i, 0, 0)),
        out_shape=jax.ShapeDtypeStruct((passages, 2 * slots, width), jnp.bfloat16),
        scratch_shapes=[pltpu.VMEM((GROUP, count // GROUP * width), jnp.bfloat16)],
        compiler_params=pltpu.CompilerParams(vmem_limit_bytes=32 * 2**20),
        cost_estimate=pl.CostEstimate(
            flops=2 * passages * slots * count * width,
            bytes_accessed=4 * passages * slots * width * 2,
            transcendentals=0,
        ),
    )(
        lengths,
        bucket_weights,
        codes.reshape(passages // STEP, STEP, slots),
        residual_codes,
        centroids,
    )


def score_kernel(query_tokens, query_rows, rows, out, best):
    passages, doubled, width = rows.shape
    slots = doubled // 2
    tokens = query_rows.shape[0]
    shards = out.shape[0]
    per_shard = tokens // shards

    def one_chunk(c, carry):
        query = query_rows[pl.ds(pl.multiple_of(c * CHUNK, CHUNK), CHUNK), :]
        for t in range(passages // TILE):
            dots = lax.dot_general(
                rows[t * TILE : (t + 1) * TILE].reshape(TILE * doubled, width),
                query,
                (((1,), (1,)), ((), ())),
                preferred_element_type=jnp.float32,
            )
            tops = jnp.max(dots.reshape(2 * TILE, slots, CHUNK), axis=1)
            best[c, 2 * TILE * t : 2 * TILE * (t + 1), :] = tops
        return carry

    lax.fori_loop(0, tokens // CHUNK, one_chunk, 0)
    out[...] = jnp.zeros_like(out)
    per_chunk = CHUNK // query_tokens
    shape = (per_chunk, CHUNK)
    own = lax.broadcasted_iota(jnp.int32, shape, 1) // query_tokens
    own = (own == lax.broadcasted_iota(jnp.int32, shape, 0)).astype(jnp.float32)
    q_local = per_shard // query_tokens

    def one_sum(c, carry):
        sums = lax.dot_general(
            own,
            best[c],
            (((1,), (1,)), ((), ())),
            precision=lax.Precision.HIGHEST,
            preferred_element_type=jnp.float32,
        )
        for s in range(CHUNK // per_shard):
            out[c * (CHUNK // per_shard) + s, :q_local, : 2 * passages] = sums[
                s * q_local : (s + 1) * q_local
            ]
        return carry

    lax.fori_loop(0, tokens // CHUNK, one_sum, 0)


def score(query_rows, rows, shards, query_tokens):
    passages, doubled, width = rows.shape
    tokens = query_rows.shape[0]
    return pl.pallas_call(
        functools.partial(score_kernel, query_tokens),
        out_shape=jax.ShapeDtypeStruct((shards, 8, 128), jnp.float32),
        scratch_shapes=[pltpu.VMEM((tokens // CHUNK, 2 * passages, CHUNK), jnp.float32)],
        compiler_params=pltpu.CompilerParams(vmem_limit_bytes=48 * 2**20),
        cost_estimate=pl.CostEstimate(
            flops=2 * tokens * passages * doubled * width,
            bytes_accessed=2 * (tokens + passages * doubled) * width,
            transcendentals=0,
        ),
    )(query_rows, rows)


def pick_kernel(passages, candidates, scores, exact_out, approx_out):
    q_local, top_k = candidates.shape
    shards, padded, lanes = scores.shape
    cand = jnp.concatenate([candidates[q : q + 1, :] for q in range(q_local)], axis=1)
    slot_count = q_local * top_k
    shape = (shards * padded, slot_count)
    source = lax.broadcasted_iota(jnp.int32, shape, 0)
    query = lax.broadcasted_iota(jnp.int32, shape, 1) // top_k
    wanted = (cand // passages) * padded + query
    hot = (source == wanted).astype(jnp.float32)
    spread = lax.dot_general(
        scores[...].reshape(shards * padded, lanes),
        hot,
        (((0,), (0,)), ((), ())),
        precision=lax.Precision.HIGHEST,
        preferred_element_type=jnp.float32,
    )
    row = lax.broadcasted_iota(jnp.int32, (lanes, slot_count), 0)
    first = 2 * (cand % passages)
    exact = jnp.sum(jnp.where(row == first, spread, 0.0), axis=0, keepdims=True)
    approx = jnp.sum(jnp.where(row == first + 1, spread, 0.0), axis=0, keepdims=True)
    for q in range(q_local):
        exact_out[q : q + 1, :] = exact[:, q * top_k : (q + 1) * top_k]
        approx_out[q : q + 1, :] = approx[:, q * top_k : (q + 1) * top_k]


def pick(candidates, scores, passages):
    shape = jax.ShapeDtypeStruct(candidates.shape, jnp.float32)
    return pl.pallas_call(
        functools.partial(pick_kernel, passages), out_shape=(shape, shape)
    )(candidates, scores)


def per_device(queries, centroids, codes, residual_codes, lengths, bucket_weights, candidates):
    shards = lax.axis_size("shard")
    passages = codes.shape[0]
    q_local, query_tokens, width = queries.shape
    own_rows = queries.reshape(1, q_local * query_tokens, width)
    sent = jnp.broadcast_to(own_rows, (shards,) + own_rows.shape[1:])
    query_rows = lax.all_to_all(sent, "shard", split_axis=0, concat_axis=0, tiled=True)
    rows = decompress(centroids, codes, residual_codes, lengths, bucket_weights)
    scores = score(query_rows.reshape(-1, width), rows, shards, query_tokens)
    back = lax.all_to_all(scores, "shard", split_axis=0, concat_axis=0, tiled=True)
    return pick(candidates, back, passages)


def solution(mesh):
    placed = (
        P(("rep", "shard"), None, None),
        P("shard", None),
        P("shard", None),
        P("shard", None, None),
        P("shard"),
        P(),
        P(("rep", "shard"), None),
    )
    return jax.shard_map(
        per_device,
        mesh=mesh,
        in_specs=placed,
        out_specs=(P(("rep", "shard"), None), P(("rep", "shard"), None)),
        check_vma=False,
    )
```

```python
import functools

import jax
import jax.numpy as jnp
from jax import lax
from jax.experimental import pallas as pl
from jax.experimental.pallas import tpu as pltpu
from jax.sharding import PartitionSpec as P

GROUP = 256
STEP = 16
CHUNK = 256
TILE = 4


def decompress_kernel(
    lengths_hbm, weights_hbm, codes_hbm, residuals_hbm, centroids_hbm, rows_out,
    lengths, weights, codes, residuals, centroids, table, sems, part_sems,
):
    passages, slots = codes.shape
    count, width = centroids.shape
    groups = count // GROUP
    small = [
        pltpu.make_async_copy(source, target, sems.at[i])
        for i, (source, target) in enumerate(
            (
                (codes_hbm, codes),
                (centroids_hbm, centroids),
                (lengths_hbm, lengths),
                (weights_hbm, weights),
            )
        )
    ]
    parts = [
        pltpu.make_async_copy(
            residuals_hbm.at[pl.ds(p, STEP)], residuals.at[pl.ds(p, STEP)], part_sems.at[p // STEP]
        )
        for p in range(0, passages, STEP)
    ]
    for copy in small + parts:
        copy.start()
    for copy in small:
        copy.wait()
    for g in range(groups):
        table[:, g * width : (g + 1) * width] = centroids[g * GROUP : (g + 1) * GROUP, :]
    code_cols = jnp.swapaxes(codes[...].astype(jnp.float32), 0, 1).astype(jnp.int32)
    lane = lax.broadcasted_iota(jnp.int32, (slots, GROUP), 1)
    token = lax.broadcasted_iota(jnp.int32, (slots, width), 0)
    for first in range(0, passages, STEP):
        parts[first // STEP].wait()
        hot = []
        high = []
        for p in range(first, first + STEP):
            code = code_cols[:, p : p + 1]
            hot.append((lane == (code % GROUP)).astype(jnp.bfloat16))
            high.append(jnp.broadcast_to(code // GROUP, (slots, width)))
        spread = jnp.dot(
            jnp.concatenate(hot, 0), table[...], preferred_element_type=jnp.float32
        )
        for p in range(first, first + STEP):
            at = p - first
            part = spread[at * slots : (at + 1) * slots]
            cent = part[:, :width]
            for g in range(1, groups):
                cent = jnp.where(high[at] == g, part[:, g * width : (g + 1) * width], cent)
            code = residuals[p]
            odd = (code & 1) == 1
            low = jnp.where(odd, weights[1], weights[0])
            top = jnp.where(odd, weights[3], weights[2])
            values = cent + jnp.where(code >= 2, top, low)
            norm = lax.rsqrt(jnp.sum(values * values, axis=-1, keepdims=True) + 1e-06)
            exact = values * norm
            live = token < lengths[p]
            exact = jnp.where(live, exact, exact[0:1, :])
            cent = jnp.where(live, cent, cent[0:1, :])
            rows_out[p, :slots, :] = exact.astype(jnp.bfloat16)
            rows_out[p, slots:, :] = cent.astype(jnp.bfloat16)


def decompress(centroids, codes, residual_codes, lengths, bucket_weights):
    passages, slots = codes.shape
    count, width = centroids.shape
    operands = (lengths, bucket_weights, codes, residual_codes, centroids)
    return pl.pallas_call(
        decompress_kernel,
        in_specs=[pl.BlockSpec(memory_space=pltpu.HBM)] * len(operands),
        out_specs=pl.BlockSpec(memory_space=pltpu.VMEM),
        out_shape=jax.ShapeDtypeStruct((passages, 2 * slots, width), jnp.bfloat16),
        scratch_shapes=[
            pltpu.SMEM(lengths.shape, lengths.dtype),
            pltpu.SMEM(bucket_weights.shape, bucket_weights.dtype),
            pltpu.VMEM(codes.shape, codes.dtype),
            pltpu.VMEM(residual_codes.shape, residual_codes.dtype),
            pltpu.VMEM(centroids.shape, centroids.dtype),
            pltpu.VMEM((GROUP, count // GROUP * width), jnp.bfloat16),
            pltpu.SemaphoreType.DMA((4,)),
            pltpu.SemaphoreType.DMA((passages // STEP,)),
        ],
        compiler_params=pltpu.CompilerParams(vmem_limit_bytes=48 * 2**20),
        cost_estimate=pl.CostEstimate(
            flops=2 * passages * slots * count * width,
            bytes_accessed=4 * passages * slots * width * 2,
            transcendentals=0,
        ),
    )(*[pltpu.with_memory_space_constraint(x, pltpu.HBM) for x in operands])


def score_kernel(query_tokens, offsets, query_rows, rows, out, best):
    passages, doubled, width = rows.shape
    slots = doubled // 2
    tokens = query_rows.shape[0]
    shards = out.shape[0]
    per_shard = tokens // shards
    me = lax.axis_index("shard")

    def one_chunk(c, carry):
        query = query_rows[pl.ds(pl.multiple_of(c * CHUNK, CHUNK), CHUNK), :]
        for t in range(passages // TILE):
            dots = lax.dot_general(
                rows[t * TILE : (t + 1) * TILE].reshape(TILE * doubled, width),
                query,
                (((1,), (1,)), ((), ())),
                preferred_element_type=jnp.float32,
            )
            tops = jnp.max(dots.reshape(2 * TILE, slots, CHUNK), axis=1)
            best[c, 2 * TILE * t : 2 * TILE * (t + 1), :] = tops
        return carry

    lax.fori_loop(0, tokens // CHUNK, one_chunk, 0)
    out[...] = jnp.zeros_like(out)
    per_chunk = CHUNK // query_tokens
    shape = (per_chunk, CHUNK)
    own = lax.broadcasted_iota(jnp.int32, shape, 1) // query_tokens
    own = (own == lax.broadcasted_iota(jnp.int32, shape, 0)).astype(jnp.float32)
    q_local = per_shard // query_tokens

    for c in range(tokens // CHUNK):
        sums = lax.dot_general(
            own,
            best[c],
            (((1,), (1,)), ((), ())),
            precision=lax.Precision.HIGHEST,
            preferred_element_type=jnp.float32,
        )
        for s in range(CHUNK // per_shard):
            source = jnp.bitwise_xor(me, offsets[c * (CHUNK // per_shard) + s])
            out[source, :q_local, : 2 * passages] = sums[s * q_local : (s + 1) * q_local]


def score(query_rows, rows, offsets, query_tokens):
    passages, doubled, width = rows.shape
    tokens = query_rows.shape[0]
    return pl.pallas_call(
        functools.partial(score_kernel, query_tokens, offsets),
        out_shape=jax.ShapeDtypeStruct((len(offsets), 8, 128), jnp.float32),
        scratch_shapes=[pltpu.VMEM((tokens // CHUNK, 2 * passages, CHUNK), jnp.float32)],
        compiler_params=pltpu.CompilerParams(vmem_limit_bytes=48 * 2**20),
        cost_estimate=pl.CostEstimate(
            flops=2 * tokens * passages * doubled * width,
            bytes_accessed=2 * (tokens + passages * doubled) * width,
            transcendentals=0,
        ),
    )(query_rows, rows)


def pick_kernel(passages, candidates, scores, exact_out, approx_out):
    q_local, top_k = candidates.shape
    shards, padded, lanes = scores.shape
    cand = jnp.concatenate([candidates[q : q + 1, :] for q in range(q_local)], axis=1)
    slot_count = q_local * top_k
    shape = (shards * padded, slot_count)
    source = lax.broadcasted_iota(jnp.int32, shape, 0)
    query = lax.broadcasted_iota(jnp.int32, shape, 1) // top_k
    wanted = (cand // passages) * padded + query
    hot = (source == wanted).astype(jnp.float32)
    spread = lax.dot_general(
        scores[...].reshape(shards * padded, lanes),
        hot,
        (((0,), (0,)), ((), ())),
        precision=lax.Precision.HIGHEST,
        preferred_element_type=jnp.float32,
    )
    row = lax.broadcasted_iota(jnp.int32, (lanes, slot_count), 0)
    first = 2 * (cand % passages)
    exact = jnp.sum(jnp.where(row == first, spread, 0.0), axis=0, keepdims=True)
    approx = jnp.sum(jnp.where(row == first + 1, spread, 0.0), axis=0, keepdims=True)
    for q in range(q_local):
        exact_out[q : q + 1, :] = exact[:, q * top_k : (q + 1) * top_k]
        approx_out[q : q + 1, :] = approx[:, q * top_k : (q + 1) * top_k]


def pick(candidates, scores, passages):
    shape = jax.ShapeDtypeStruct(candidates.shape, jnp.float32)
    return pl.pallas_call(
        functools.partial(pick_kernel, passages), out_shape=(shape, shape)
    )(candidates, scores)


def exchange(block, steps, shards):
    others = [
        lax.ppermute(block, "shard", [(i, i ^ step) for i in range(shards)]) for step in steps
    ]
    return jnp.concatenate([block] + others, axis=0)


def per_device(queries, centroids, codes, residual_codes, lengths, bucket_weights, candidates):
    shards = lax.axis_size("shard")
    passages = codes.shape[0]
    q_local, query_tokens, width = queries.shape
    query_rows = queries.reshape(q_local * query_tokens, width)
    offsets = [0]
    stride = shards
    while stride > 1:
        ways = 4 if stride % 4 == 0 else 2
        stride //= ways
        steps = [stride * k for k in range(1, ways)]
        query_rows = exchange(query_rows, steps, shards)
        offsets = [k ^ at for k in [0] + steps for at in offsets]
        if stride > 1:
            query_rows, codes = lax.optimization_barrier((query_rows, codes))
    rows = decompress(centroids, codes, residual_codes, lengths, bucket_weights)
    scores = score(query_rows, rows, offsets, query_tokens)
    back = lax.all_to_all(scores, "shard", split_axis=0, concat_axis=0, tiled=True)
    return pick(candidates, back, passages)


def solution(mesh):
    placed = (
        P(("rep", "shard"), None, None),
        P("shard", None),
        P("shard", None),
        P("shard", None, None),
        P("shard"),
        P(),
        P(("rep", "shard"), None),
    )
    return jax.shard_map(
        per_device,
        mesh=mesh,
        in_specs=placed,
        out_specs=(P(("rep", "shard"), None), P(("rep", "shard"), None)),
        check_vma=False,
    )
```

```python
import functools

import jax
import jax.numpy as jnp
from jax import lax
from jax.experimental import pallas as pl
from jax.experimental.pallas import tpu as pltpu
from jax.sharding import PartitionSpec as P

GROUP = 256
STEP = 16
META = 16
LANES = 128
PACK = 8
CUTS = (0, 32, 48)


def decompress_kernel(
    lengths_hbm, weights_hbm, codes_hbm, residuals_hbm, centroids_hbm, rows_out,
    lengths, weights, codes, residuals, centroids, table, sems, part_sems,
):
    passages, slots = codes.shape
    count, width = centroids.shape
    groups = count // GROUP
    small = [
        pltpu.make_async_copy(source, target, sems.at[i])
        for i, (source, target) in enumerate(
            (
                (codes_hbm, codes),
                (centroids_hbm, centroids),
                (lengths_hbm, lengths),
                (weights_hbm, weights),
            )
        )
    ]
    parts = [
        pltpu.make_async_copy(
            residuals_hbm.at[pl.ds(p, STEP)], residuals.at[pl.ds(p, STEP)], part_sems.at[p // STEP]
        )
        for p in range(0, passages, STEP)
    ]
    for copy in small + parts:
        copy.start()
    for copy in small:
        copy.wait()
    for g in range(groups):
        table[:, g * width : (g + 1) * width] = centroids[g * GROUP : (g + 1) * GROUP, :]
    code_cols = jnp.swapaxes(codes[...].astype(jnp.float32), 0, 1).astype(jnp.int32)
    lane = lax.broadcasted_iota(jnp.int32, (slots, GROUP), 1)
    token = lax.broadcasted_iota(jnp.int32, (slots, width), 0)
    for first in range(0, passages, STEP):
        parts[first // STEP].wait()
        hot = []
        high = []
        for p in range(first, first + STEP):
            code = code_cols[:, p : p + 1]
            hot.append((lane == (code % GROUP)).astype(jnp.bfloat16))
            high.append(jnp.broadcast_to(code // GROUP, (slots, width)))
        spread = jnp.dot(
            jnp.concatenate(hot, 0), table[...], preferred_element_type=jnp.float32
        )
        for p in range(first, first + STEP):
            at = p - first
            part = spread[at * slots : (at + 1) * slots]
            cent = part[:, :width]
            for g in range(1, groups):
                cent = jnp.where(high[at] == g, part[:, g * width : (g + 1) * width], cent)
            code = residuals[p]
            odd = (code & 1) == 1
            low = jnp.where(odd, weights[1], weights[0])
            top = jnp.where(odd, weights[3], weights[2])
            values = cent + jnp.where(code >= 2, top, low)
            norm = lax.rsqrt(jnp.sum(values * values, axis=-1, keepdims=True) + 1e-06)
            exact = values * norm
            live = token < lengths[p]
            exact = jnp.where(live, exact, exact[0:1, :])
            cent = jnp.where(live, cent, cent[0:1, :])
            rows_out[p, :slots, :] = exact.astype(jnp.bfloat16)
            rows_out[p, slots:, :] = cent.astype(jnp.bfloat16)


def decompress(centroids, codes, residual_codes, lengths, bucket_weights):
    passages, slots = codes.shape
    count, width = centroids.shape
    operands = (lengths, bucket_weights, codes, residual_codes, centroids)
    return pl.pallas_call(
        decompress_kernel,
        in_specs=[pl.BlockSpec(memory_space=pltpu.HBM)] * len(operands),
        out_specs=pl.BlockSpec(memory_space=pltpu.VMEM),
        out_shape=jax.ShapeDtypeStruct((passages, 2 * slots, width), jnp.bfloat16),
        scratch_shapes=[
            pltpu.SMEM(lengths.shape, lengths.dtype),
            pltpu.SMEM(bucket_weights.shape, bucket_weights.dtype),
            pltpu.VMEM(codes.shape, codes.dtype),
            pltpu.VMEM(residual_codes.shape, residual_codes.dtype),
            pltpu.VMEM(centroids.shape, centroids.dtype),
            pltpu.VMEM((GROUP, count // GROUP * width), jnp.bfloat16),
            pltpu.SemaphoreType.DMA((4,)),
            pltpu.SemaphoreType.DMA((passages // STEP,)),
        ],
        compiler_params=pltpu.CompilerParams(vmem_limit_bytes=48 * 2**20),
        cost_estimate=pl.CostEstimate(
            flops=2 * passages * slots * count * width,
            bytes_accessed=4 * passages * slots * width * 2,
            transcendentals=0,
        ),
    )(*[pltpu.with_memory_space_constraint(x, pltpu.HBM) for x in operands])


def plan_kernel(shards, cap, passages, queries_hbm, candidates_hbm, block, plan, candidates, query_sem, cand_sem):
    q_local, top_k = candidates.shape
    tokens = queries_hbm.shape[0]
    send_queries = pltpu.make_async_copy(queries_hbm, block.at[pl.ds(0, tokens)], query_sem)
    get_candidates = pltpu.make_async_copy(candidates_hbm, candidates, cand_sem)
    get_candidates.start()
    send_queries.start()
    get_candidates.wait()
    slots = q_local * top_k
    per_row = shards // META
    cand = jnp.concatenate([candidates[q : q + 1, :] for q in range(q_local)], axis=1)
    target = cand // passages
    value = lax.broadcasted_iota(jnp.int32, (1, slots), 1) // top_k * passages + cand % passages + 1
    square = (slots, slots)
    wide = jnp.broadcast_to(target.astype(jnp.float32), square)
    earlier = lax.broadcasted_iota(jnp.int32, square, 0) < lax.broadcasted_iota(
        jnp.int32, square, 1
    )
    same = (jnp.swapaxes(wide, 0, 1) == wide) & earlier
    rank = jnp.sum(same.astype(jnp.int32), axis=0, keepdims=True)
    row = lax.broadcasted_iota(jnp.int32, (META, slots), 0)
    left = jnp.where(row == target // per_row, value.astype(jnp.float32), 0.0)
    lane = lax.broadcasted_iota(jnp.int32, (LANES, slots), 0)
    right = (lane == target % per_row * cap + rank).astype(jnp.float32)
    lists = lax.dot_general(
        left.astype(jnp.bfloat16),
        right.astype(jnp.bfloat16),
        (((1,), (1,)), ((), ())),
        preferred_element_type=jnp.float32,
    )
    block[tokens:, :] = lists.astype(jnp.bfloat16)
    plan[0:1, :] = target
    plan[1:2, :] = rank
    send_queries.wait()


def make_plan(queries, candidates, shards, cap, passages):
    tokens, width = queries.shape
    operands = (queries, candidates)
    return pl.pallas_call(
        functools.partial(plan_kernel, shards, cap, passages),
        in_specs=[pl.BlockSpec(memory_space=pltpu.HBM)] * 2,
        out_specs=[pl.BlockSpec(memory_space=pltpu.VMEM)] * 2,
        out_shape=(
            jax.ShapeDtypeStruct((tokens + META, width), jnp.bfloat16),
            jax.ShapeDtypeStruct((8, candidates.size), jnp.int32),
        ),
        scratch_shapes=[
            pltpu.VMEM(candidates.shape, candidates.dtype),
            pltpu.SemaphoreType.DMA,
            pltpu.SemaphoreType.DMA,
        ],
    )(*[pltpu.with_memory_space_constraint(x, pltpu.HBM) for x in operands])


def exact_dot(a, b, dims):
    return lax.dot_general(
        a,
        b,
        (dims, ((), ())),
        precision=lax.Precision.HIGHEST,
        preferred_element_type=jnp.float32,
    )


def score_kernel(query_tokens, cap, offsets, blocks, rows, out, listed, steps, tops, sem):
    passages, doubled, width = rows.shape
    slots = doubled // 2
    shards, block_rows, _ = blocks.shape
    per_row = shards // META
    me = lax.axis_index("shard")
    pairs = shards * cap
    max_steps = listed.shape[0]

    lists = blocks[:, block_rows - META :, :].reshape(shards * META, LANES)
    shape = (pairs, shards * META)
    pair = lax.broadcasted_iota(jnp.int32, shape, 0)
    wanted = pair // cap * META + me // per_row
    pick = (lax.broadcasted_iota(jnp.int32, shape, 1) == wanted).astype(jnp.bfloat16)
    found = jnp.dot(pick, lists, preferred_element_type=jnp.float32)
    shape = (pairs, LANES)
    lane = me % per_row * cap + lax.broadcasted_iota(jnp.int32, shape, 0) % cap
    own = lax.broadcasted_iota(jnp.int32, shape, 1) == lane
    column = jnp.sum(jnp.where(own, found, 0.0), axis=1, keepdims=True)
    wide = jnp.broadcast_to(column, shape)
    code_row = jnp.swapaxes(wide, 0, 1)[0:1, :].astype(jnp.int32)
    code_col = wide.astype(jnp.int32)

    def passage_of(code):
        return jnp.where(code > 0, (code - 1) % passages, passages)

    valid = code_row > 0
    p_row = passage_of(code_row)
    p_col = passage_of(code_col)[:, 0:1]
    square = (pairs, pairs)
    earlier = lax.broadcasted_iota(jnp.int32, square, 0) < lax.broadcasted_iota(
        jnp.int32, square, 1
    )
    rank = jnp.sum(((p_col == p_row) & earlier).astype(jnp.int32), axis=0, keepdims=True)
    shape = (passages, pairs)
    p_iota = lax.broadcasted_iota(jnp.int32, shape, 0)
    count = jnp.sum((p_iota == p_row).astype(jnp.int32), axis=1, keepdims=True)
    need = (count + PACK - 1) // PACK
    start = jnp.sum(jnp.where(p_iota < p_row, need, 0), axis=0, keepdims=True)
    step_row = jnp.where(valid, start + rank // PACK, max_steps)
    place_row = rank % PACK
    pair_row = lax.broadcasted_iota(jnp.int32, (1, pairs), 1)
    query_row = pair_row // cap * (block_rows // 16) + (code_row - 1) // passages * (
        query_tokens // 16
    )
    shape = (max_steps, pairs)
    in_step = lax.broadcasted_iota(jnp.int32, shape, 0) == step_row
    at_place = lax.broadcasted_iota(jnp.int32, (LANES, pairs), 0) == place_row
    queries = exact_dot(
        jnp.where(in_step, query_row.astype(jnp.float32), 0.0),
        at_place.astype(jnp.float32),
        ((1,), (1,)),
    )
    first = in_step & (place_row == 0)
    passage = jnp.sum(jnp.where(first, p_row, 0), axis=1, keepdims=True)
    lane = lax.broadcasted_iota(jnp.int32, (max_steps, LANES), 1)
    total = jnp.sum(need, axis=0, keepdims=True)
    table = jnp.where(lane == PACK, passage, queries.astype(jnp.int32))
    listed[...] = jnp.where(lane == PACK + 1, total, table)
    copy = pltpu.make_async_copy(listed, steps, sem)
    copy.start()
    tops[...] = jnp.zeros_like(tops)
    copy.wait()

    flat = blocks.reshape(shards * block_rows, width)

    def one_step(step):
        packed = [
            flat[pl.ds(pl.multiple_of(steps[step, k] * 16, 16), query_tokens), :]
            for k in range(PACK)
        ]
        dots = lax.dot_general(
            rows[steps[step, PACK]],
            jnp.concatenate(packed, axis=0),
            (((1,), (1,)), ((), ())),
            preferred_element_type=jnp.float32,
        )
        best = jnp.max(dots.reshape(2, slots, PACK * query_tokens), axis=1)
        tops[step : step + 1, :] = best[0:1]
        tops[max_steps + step : max_steps + step + 1, :] = best[1:2]

    taken = steps[0, PACK + 1]
    for begin, end in zip(CUTS, CUTS[1:] + (max_steps,)):

        @pl.when(taken > begin)
        def _():
            for step in range(begin, end):
                one_step(step)

    shape = (PACK, PACK * query_tokens)
    own = lax.broadcasted_iota(jnp.int32, shape, 1) // query_tokens
    own = (own == lax.broadcasted_iota(jnp.int32, shape, 0)).astype(jnp.float32)
    sums = exact_dot(own, tops[...], ((1,), (1,)))
    both = jnp.concatenate([sums[:, :max_steps], sums[:, max_steps:]], axis=0)
    spread = exact_dot(both, in_step.astype(jnp.float32), ((1,), (0,)))
    here = lax.broadcasted_iota(jnp.int32, (PACK, pairs), 0) == place_row
    exact = jnp.sum(jnp.where(here, spread[:PACK], 0.0), axis=0, keepdims=True)
    approx = jnp.sum(jnp.where(here, spread[PACK:], 0.0), axis=0, keepdims=True)
    shape = (shards, 2 * pairs)
    pair = lax.broadcasted_iota(jnp.int32, shape, 1)
    from_shard = pair % pairs // cap == lax.broadcasted_iota(jnp.int32, shape, 0)
    scores = jnp.where(from_shard, jnp.concatenate([exact, approx], axis=1), 0.0)
    shape = (LANES, 2 * pairs)
    pair = lax.broadcasted_iota(jnp.int32, shape, 1)
    lane = pair // pairs * (LANES // 2) + pair % cap
    to_lane = (lax.broadcasted_iota(jnp.int32, shape, 0) == lane).astype(jnp.float32)
    back = exact_dot(scores, to_lane, ((1,), (1,)))
    out[...] = jnp.zeros_like(out)
    for k, offset in enumerate(offsets):
        out[jnp.bitwise_xor(me, offset), 0:1, :] = back[k : k + 1, :]


def score(blocks, rows, offsets, query_tokens, cap):
    passages, doubled, width = rows.shape
    shards = len(offsets)
    max_steps = -(-(shards * cap + (PACK - 1) * passages) // (8 * PACK)) * 8
    return pl.pallas_call(
        functools.partial(score_kernel, query_tokens, cap, offsets),
        out_shape=jax.ShapeDtypeStruct((shards, 8, LANES), jnp.float32),
        scratch_shapes=[
            pltpu.VMEM((max_steps, LANES), jnp.int32),
            pltpu.SMEM((max_steps, LANES), jnp.int32),
            pltpu.VMEM((2 * max_steps, PACK * query_tokens), jnp.float32),
            pltpu.SemaphoreType.DMA,
        ],
        compiler_params=pltpu.CompilerParams(vmem_limit_bytes=48 * 2**20),
        cost_estimate=pl.CostEstimate(
            flops=2 * max_steps * PACK * query_tokens * doubled * width,
            bytes_accessed=2 * (blocks.size + rows.size),
            transcendentals=0,
        ),
    )(blocks, rows)


def pick_kernel(plan, scores, exact_out, approx_out):
    q_local, top_k = exact_out.shape
    shards, padded, lanes = scores.shape
    slots = q_local * top_k
    target = plan[0:1, :]
    rank = plan[1:2, :]
    source = lax.broadcasted_iota(jnp.int32, (shards * padded, slots), 0)
    hot = (source == target * padded).astype(jnp.float32)
    spread = exact_dot(scores[...].reshape(shards * padded, lanes), hot, ((0,), (0,)))
    lane = lax.broadcasted_iota(jnp.int32, (lanes, slots), 0)
    exact = jnp.sum(jnp.where(lane == rank, spread, 0.0), axis=0, keepdims=True)
    approx = jnp.sum(jnp.where(lane == rank + lanes // 2, spread, 0.0), axis=0, keepdims=True)
    for q in range(q_local):
        exact_out[q : q + 1, :] = exact[:, q * top_k : (q + 1) * top_k]
        approx_out[q : q + 1, :] = approx[:, q * top_k : (q + 1) * top_k]


def pick(plan, scores, shape):
    result = jax.ShapeDtypeStruct(shape, jnp.float32)
    return pl.pallas_call(pick_kernel, out_shape=(result, result))(plan, scores)


def exchange(block, steps, shards):
    others = [
        lax.ppermute(block, "shard", [(i, i ^ step) for i in range(shards)]) for step in steps
    ]
    return jnp.concatenate([block] + others, axis=0)


def per_device(queries, centroids, codes, residual_codes, lengths, bucket_weights, candidates):
    shards = lax.axis_size("shard")
    passages = codes.shape[0]
    q_local, query_tokens, width = queries.shape
    cap = max(2, 2 * candidates.size // shards)
    block, plan = make_plan(
        queries.reshape(q_local * query_tokens, width), candidates, shards, cap, passages
    )
    block_rows = block.shape[0]
    offsets = [0]
    stride = shards
    while stride > 1:
        ways = 4 if stride % 4 == 0 else 2
        stride //= ways
        steps = [stride * k for k in range(1, ways)]
        block = exchange(block, steps, shards)
        offsets = [k ^ at for k in [0] + steps for at in offsets]
        if stride > 1:
            block, codes = lax.optimization_barrier((block, codes))
    rows = decompress(centroids, codes, residual_codes, lengths, bucket_weights)
    scores = score(block.reshape(shards, block_rows, width), rows, offsets, query_tokens, cap)
    back = lax.all_to_all(scores, "shard", split_axis=0, concat_axis=0, tiled=True)
    return pick(plan, back, candidates.shape)


def solution(mesh):
    placed = (
        P(("rep", "shard"), None, None),
        P("shard", None),
        P("shard", None),
        P("shard", None, None),
        P("shard"),
        P(),
        P(("rep", "shard"), None),
    )
    return jax.shard_map(
        per_device,
        mesh=mesh,
        in_specs=placed,
        out_specs=(P(("rep", "shard"), None), P(("rep", "shard"), None)),
        check_vma=False,
    )
```

```python
import functools

import jax
import jax.numpy as jnp
from jax import lax
from jax.experimental import pallas as pl
from jax.experimental.pallas import tpu as pltpu
from jax.sharding import PartitionSpec as P

GROUP = 256
STEP = 16
META = 16
LANES = 128
PACK = 8
CUTS = (0, 32, 48)


def decompress_kernel(
    lengths_hbm, weights_hbm, codes_hbm, residuals_hbm, centroids_hbm, rows_out,
    lengths, weights, codes, residuals, centroids, table, sems, part_sems,
):
    passages, slots = codes.shape
    count, width = centroids.shape
    groups = count // GROUP
    small = [
        pltpu.make_async_copy(source, target, sems.at[i])
        for i, (source, target) in enumerate(
            (
                (codes_hbm, codes),
                (centroids_hbm, centroids),
                (lengths_hbm, lengths),
                (weights_hbm, weights),
            )
        )
    ]
    parts = [
        pltpu.make_async_copy(
            residuals_hbm.at[pl.ds(p, STEP)], residuals.at[pl.ds(p, STEP)], part_sems.at[p // STEP]
        )
        for p in range(0, passages, STEP)
    ]
    for copy in small + parts:
        copy.start()
    for copy in small:
        copy.wait()
    for g in range(groups):
        table[:, g * width : (g + 1) * width] = centroids[g * GROUP : (g + 1) * GROUP, :]
    code_cols = jnp.swapaxes(codes[...].astype(jnp.float32), 0, 1).astype(jnp.int32)
    lane = lax.broadcasted_iota(jnp.int32, (slots, GROUP), 1)
    token = lax.broadcasted_iota(jnp.int32, (slots, width), 0)
    for first in range(0, passages, STEP):
        parts[first // STEP].wait()
        hot = []
        high = []
        for p in range(first, first + STEP):
            code = code_cols[:, p : p + 1]
            hot.append((lane == (code % GROUP)).astype(jnp.bfloat16))
            high.append(jnp.broadcast_to(code // GROUP, (slots, width)))
        spread = jnp.dot(
            jnp.concatenate(hot, 0), table[...], preferred_element_type=jnp.float32
        )
        for p in range(first, first + STEP):
            at = p - first
            part = spread[at * slots : (at + 1) * slots]
            cent = part[:, :width]
            for g in range(1, groups):
                cent = jnp.where(high[at] == g, part[:, g * width : (g + 1) * width], cent)
            code = residuals[p]
            odd = (code & 1) == 1
            low = jnp.where(odd, weights[1], weights[0])
            top = jnp.where(odd, weights[3], weights[2])
            values = cent + jnp.where(code >= 2, top, low)
            norm = lax.rsqrt(jnp.sum(values * values, axis=-1, keepdims=True) + 1e-06)
            exact = values * norm
            live = token < lengths[p]
            exact = jnp.where(live, exact, exact[0:1, :])
            cent = jnp.where(live, cent, cent[0:1, :])
            rows_out[p, :slots, :] = exact.astype(jnp.bfloat16)
            rows_out[p, slots:, :] = cent.astype(jnp.bfloat16)


def decompress(centroids, codes, residual_codes, lengths, bucket_weights):
    passages, slots = codes.shape
    count, width = centroids.shape
    operands = (lengths, bucket_weights, codes, residual_codes, centroids)
    return pl.pallas_call(
        decompress_kernel,
        in_specs=[pl.BlockSpec(memory_space=pltpu.HBM)] * len(operands),
        out_specs=pl.BlockSpec(memory_space=pltpu.VMEM),
        out_shape=jax.ShapeDtypeStruct((passages, 2 * slots, width), jnp.bfloat16),
        scratch_shapes=[
            pltpu.SMEM(lengths.shape, lengths.dtype),
            pltpu.SMEM(bucket_weights.shape, bucket_weights.dtype),
            pltpu.VMEM(codes.shape, codes.dtype),
            pltpu.VMEM(residual_codes.shape, residual_codes.dtype),
            pltpu.VMEM(centroids.shape, centroids.dtype),
            pltpu.VMEM((GROUP, count // GROUP * width), jnp.bfloat16),
            pltpu.SemaphoreType.DMA((4,)),
            pltpu.SemaphoreType.DMA((passages // STEP,)),
        ],
        compiler_params=pltpu.CompilerParams(vmem_limit_bytes=48 * 2**20),
        cost_estimate=pl.CostEstimate(
            flops=2 * passages * slots * count * width,
            bytes_accessed=4 * passages * slots * width * 2,
            transcendentals=0,
        ),
    )(*[pltpu.with_memory_space_constraint(x, pltpu.HBM) for x in operands])


def plan_kernel(shards, cap, passages, queries_hbm, candidates_hbm, block, plan, candidates, query_sem, cand_sem):
    q_local, top_k = candidates.shape
    tokens = queries_hbm.shape[0]
    send_queries = pltpu.make_async_copy(queries_hbm, block.at[pl.ds(0, tokens)], query_sem)
    get_candidates = pltpu.make_async_copy(candidates_hbm, candidates, cand_sem)
    get_candidates.start()
    send_queries.start()
    get_candidates.wait()
    slots = q_local * top_k
    per_row = shards // META
    cand = jnp.concatenate([candidates[q : q + 1, :] for q in range(q_local)], axis=1)
    target = cand // passages
    value = lax.broadcasted_iota(jnp.int32, (1, slots), 1) // top_k * passages + cand % passages + 1
    square = (slots, slots)
    wide = jnp.broadcast_to(target.astype(jnp.float32), square)
    earlier = lax.broadcasted_iota(jnp.int32, square, 0) < lax.broadcasted_iota(
        jnp.int32, square, 1
    )
    same = (jnp.swapaxes(wide, 0, 1) == wide) & earlier
    rank = jnp.sum(same.astype(jnp.int32), axis=0, keepdims=True)
    row = lax.broadcasted_iota(jnp.int32, (META, slots), 0)
    left = jnp.where(row == target // per_row, value.astype(jnp.float32), 0.0)
    lane = lax.broadcasted_iota(jnp.int32, (LANES, slots), 0)
    right = (lane == target % per_row * cap + rank).astype(jnp.float32)
    lists = lax.dot_general(
        left.astype(jnp.bfloat16),
        right.astype(jnp.bfloat16),
        (((1,), (1,)), ((), ())),
        preferred_element_type=jnp.float32,
    )
    block[tokens:, :] = lists.astype(jnp.bfloat16)
    plan[0:1, :] = target
    plan[1:2, :] = rank
    send_queries.wait()


def make_plan(queries, candidates, shards, cap, passages):
    tokens, width = queries.shape
    operands = (queries, candidates)
    return pl.pallas_call(
        functools.partial(plan_kernel, shards, cap, passages),
        in_specs=[pl.BlockSpec(memory_space=pltpu.HBM)] * 2,
        out_specs=[pl.BlockSpec(memory_space=pltpu.VMEM)] * 2,
        out_shape=(
            pltpu.VMEM((tokens + META, width), jnp.bfloat16),
            pltpu.VMEM((8, candidates.size), jnp.int32),
        ),
        scratch_shapes=[
            pltpu.VMEM(candidates.shape, candidates.dtype),
            pltpu.SemaphoreType.DMA,
            pltpu.SemaphoreType.DMA,
        ],
    )(*[pltpu.with_memory_space_constraint(x, pltpu.HBM) for x in operands])


def exact_dot(a, b, dims):
    return lax.dot_general(
        a,
        b,
        (dims, ((), ())),
        precision=lax.Precision.HIGHEST,
        preferred_element_type=jnp.float32,
    )


def score_kernel(query_tokens, cap, offsets, blocks, rows, out, listed, steps, tops, sem):
    passages, doubled, width = rows.shape
    slots = doubled // 2
    shards, block_rows, _ = blocks.shape
    per_row = shards // META
    me = lax.axis_index("shard")
    pairs = shards * cap
    max_steps = listed.shape[0]

    lists = blocks[:, block_rows - META :, :].reshape(shards * META, LANES)
    shape = (pairs, shards * META)
    pair = lax.broadcasted_iota(jnp.int32, shape, 0)
    wanted = pair // cap * META + me // per_row
    pick = (lax.broadcasted_iota(jnp.int32, shape, 1) == wanted).astype(jnp.bfloat16)
    found = jnp.dot(pick, lists, preferred_element_type=jnp.float32)
    shape = (pairs, LANES)
    lane = me % per_row * cap + lax.broadcasted_iota(jnp.int32, shape, 0) % cap
    own = lax.broadcasted_iota(jnp.int32, shape, 1) == lane
    column = jnp.sum(jnp.where(own, found, 0.0), axis=1, keepdims=True)
    wide = jnp.broadcast_to(column, shape)
    code_row = jnp.swapaxes(wide, 0, 1)[0:1, :].astype(jnp.int32)
    code_col = wide.astype(jnp.int32)

    def passage_of(code):
        return jnp.where(code > 0, (code - 1) % passages, passages)

    valid = code_row > 0
    p_row = passage_of(code_row)
    p_col = passage_of(code_col)[:, 0:1]
    square = (pairs, pairs)
    earlier = lax.broadcasted_iota(jnp.int32, square, 0) < lax.broadcasted_iota(
        jnp.int32, square, 1
    )
    rank = jnp.sum(((p_col == p_row) & earlier).astype(jnp.int32), axis=0, keepdims=True)
    shape = (passages, pairs)
    p_iota = lax.broadcasted_iota(jnp.int32, shape, 0)
    count = jnp.sum((p_iota == p_row).astype(jnp.int32), axis=1, keepdims=True)
    need = (count + PACK - 1) // PACK
    start = jnp.sum(jnp.where(p_iota < p_row, need, 0), axis=0, keepdims=True)
    step_row = jnp.where(valid, start + rank // PACK, max_steps)
    place_row = rank % PACK
    pair_row = lax.broadcasted_iota(jnp.int32, (1, pairs), 1)
    query_row = pair_row // cap * (block_rows // 16) + (code_row - 1) // passages * (
        query_tokens // 16
    )
    shape = (max_steps, pairs)
    in_step = lax.broadcasted_iota(jnp.int32, shape, 0) == step_row
    at_place = lax.broadcasted_iota(jnp.int32, (LANES, pairs), 0) == place_row
    queries = exact_dot(
        jnp.where(in_step, query_row.astype(jnp.float32), 0.0),
        at_place.astype(jnp.float32),
        ((1,), (1,)),
    )
    first = in_step & (place_row == 0)
    passage = jnp.sum(jnp.where(first, p_row, 0), axis=1, keepdims=True)
    lane = lax.broadcasted_iota(jnp.int32, (max_steps, LANES), 1)
    total = jnp.sum(need, axis=0, keepdims=True)
    table = jnp.where(lane == PACK, passage, queries.astype(jnp.int32))
    listed[...] = jnp.where(lane == PACK + 1, total, table)
    copy = pltpu.make_async_copy(listed, steps, sem)
    copy.start()
    tops[...] = jnp.zeros_like(tops)
    copy.wait()

    flat = blocks.reshape(shards * block_rows, width)

    def one_step(step):
        packed = [
            flat[pl.ds(pl.multiple_of(steps[step, k] * 16, 16), query_tokens), :]
            for k in range(PACK)
        ]
        dots = lax.dot_general(
            rows[steps[step, PACK]],
            jnp.concatenate(packed, axis=0),
            (((1,), (1,)), ((), ())),
            preferred_element_type=jnp.float32,
        )
        best = jnp.max(dots.reshape(2, slots, PACK * query_tokens), axis=1)
        tops[step : step + 1, :] = best[0:1]
        tops[max_steps + step : max_steps + step + 1, :] = best[1:2]

    taken = steps[0, PACK + 1]
    for begin, end in zip(CUTS, CUTS[1:] + (max_steps,)):

        @pl.when(taken > begin)
        def _():
            for step in range(begin, end):
                one_step(step)

    shape = (PACK, PACK * query_tokens)
    own = lax.broadcasted_iota(jnp.int32, shape, 1) // query_tokens
    own = (own == lax.broadcasted_iota(jnp.int32, shape, 0)).astype(jnp.float32)
    sums = exact_dot(own, tops[...], ((1,), (1,)))
    both = jnp.concatenate([sums[:, :max_steps], sums[:, max_steps:]], axis=0)
    spread = exact_dot(both, in_step.astype(jnp.float32), ((1,), (0,)))
    here = lax.broadcasted_iota(jnp.int32, (PACK, pairs), 0) == place_row
    exact = jnp.sum(jnp.where(here, spread[:PACK], 0.0), axis=0, keepdims=True)
    approx = jnp.sum(jnp.where(here, spread[PACK:], 0.0), axis=0, keepdims=True)
    shape = (shards, 2 * pairs)
    pair = lax.broadcasted_iota(jnp.int32, shape, 1)
    from_shard = pair % pairs // cap == lax.broadcasted_iota(jnp.int32, shape, 0)
    scores = jnp.where(from_shard, jnp.concatenate([exact, approx], axis=1), 0.0)
    shape = (LANES, 2 * pairs)
    pair = lax.broadcasted_iota(jnp.int32, shape, 1)
    lane = pair // pairs * (LANES // 2) + pair % cap
    to_lane = (lax.broadcasted_iota(jnp.int32, shape, 0) == lane).astype(jnp.float32)
    back = exact_dot(scores, to_lane, ((1,), (1,)))
    out[...] = jnp.zeros_like(out)
    for k, offset in enumerate(offsets):
        out[jnp.bitwise_xor(me, offset), 0:1, :] = back[k : k + 1, :]


def score(blocks, rows, offsets, query_tokens, cap):
    passages, doubled, width = rows.shape
    shards = len(offsets)
    max_steps = -(-(shards * cap + (PACK - 1) * passages) // (8 * PACK)) * 8
    return pl.pallas_call(
        functools.partial(score_kernel, query_tokens, cap, offsets),
        out_shape=jax.ShapeDtypeStruct((shards, 8, LANES), jnp.float32),
        scratch_shapes=[
            pltpu.VMEM((max_steps, LANES), jnp.int32),
            pltpu.SMEM((max_steps, LANES), jnp.int32),
            pltpu.VMEM((2 * max_steps, PACK * query_tokens), jnp.float32),
            pltpu.SemaphoreType.DMA,
        ],
        compiler_params=pltpu.CompilerParams(vmem_limit_bytes=48 * 2**20),
        cost_estimate=pl.CostEstimate(
            flops=2 * max_steps * PACK * query_tokens * doubled * width,
            bytes_accessed=2 * (blocks.size + rows.size),
            transcendentals=0,
        ),
    )(blocks, rows)


def pick_kernel(plan, scores, exact_out, approx_out):
    q_local, top_k = exact_out.shape
    shards, padded, lanes = scores.shape
    slots = q_local * top_k
    target = plan[0:1, :]
    rank = plan[1:2, :]
    source = lax.broadcasted_iota(jnp.int32, (shards * padded, slots), 0)
    hot = (source == target * padded).astype(jnp.float32)
    spread = exact_dot(scores[...].reshape(shards * padded, lanes), hot, ((0,), (0,)))
    lane = lax.broadcasted_iota(jnp.int32, (lanes, slots), 0)
    exact = jnp.sum(jnp.where(lane == rank, spread, 0.0), axis=0, keepdims=True)
    approx = jnp.sum(jnp.where(lane == rank + lanes // 2, spread, 0.0), axis=0, keepdims=True)
    for q in range(q_local):
        exact_out[q : q + 1, :] = exact[:, q * top_k : (q + 1) * top_k]
        approx_out[q : q + 1, :] = approx[:, q * top_k : (q + 1) * top_k]


def pick(plan, scores, shape):
    result = jax.ShapeDtypeStruct(shape, jnp.float32)
    operands = [pltpu.with_memory_space_constraint(x, pltpu.VMEM) for x in (plan, scores)]
    return pl.pallas_call(pick_kernel, out_shape=(result, result))(*operands)


def exchange(block, steps, shards):
    others = [
        lax.ppermute(block, "shard", [(i, i ^ step) for i in range(shards)]) for step in steps
    ]
    return jnp.concatenate([block] + others, axis=0)


def per_device(queries, centroids, codes, residual_codes, lengths, bucket_weights, candidates):
    shards = lax.axis_size("shard")
    passages = codes.shape[0]
    q_local, query_tokens, width = queries.shape
    cap = max(2, 2 * candidates.size // shards)
    block, plan = make_plan(
        queries.reshape(q_local * query_tokens, width), candidates, shards, cap, passages
    )
    block_rows = block.shape[0]
    offsets = [0]
    stride = shards
    while stride > 1:
        ways = 4 if stride % 4 == 0 else 2
        stride //= ways
        steps = [stride * k for k in range(1, ways)]
        block = exchange(block, steps, shards)
        offsets = [k ^ at for k in [0] + steps for at in offsets]
        if stride > 1:
            block, codes = lax.optimization_barrier((block, codes))
    rows = decompress(centroids, codes, residual_codes, lengths, bucket_weights)
    scores = score(block.reshape(shards, block_rows, width), rows, offsets, query_tokens, cap)
    back = lax.all_to_all(scores, "shard", split_axis=0, concat_axis=0, tiled=True)
    return pick(plan, back, candidates.shape)


def solution(mesh):
    placed = (
        P(("rep", "shard"), None, None),
        P("shard", None),
        P("shard", None),
        P("shard", None, None),
        P("shard"),
        P(),
        P(("rep", "shard"), None),
    )
    return jax.shard_map(
        per_device,
        mesh=mesh,
        in_specs=placed,
        out_specs=(P(("rep", "shard"), None), P(("rep", "shard"), None)),
        check_vma=False,
    )
```

```python
import functools

import jax
import jax.numpy as jnp
from jax import lax
from jax.experimental import pallas as pl
from jax.experimental.pallas import tpu as pltpu
from jax.sharding import PartitionSpec as P

GROUP = 256
STEP = 16
META = 16
LANES = 128
PACK = 8
CUTS = (0, 32, 48)


def fetch_kernel(*refs):
    count = len(refs) // 2
    copies = [
        pltpu.make_async_copy(refs[i], refs[count + i], refs[-1].at[i]) for i in range(count)
    ]
    for copy in copies:
        copy.start()
    for copy in copies:
        copy.wait()


def fetch(*arrays):
    return pl.pallas_call(
        fetch_kernel,
        in_specs=[pl.BlockSpec(memory_space=pltpu.HBM)] * len(arrays),
        out_specs=[pl.BlockSpec(memory_space=pltpu.VMEM)] * len(arrays),
        out_shape=[pltpu.VMEM(x.shape, x.dtype) for x in arrays],
        scratch_shapes=[pltpu.SemaphoreType.DMA((len(arrays),))],
        compiler_params=pltpu.CompilerParams(vmem_limit_bytes=16 * 2**20),
        cost_estimate=pl.CostEstimate(
            flops=0, bytes_accessed=2 * sum(x.nbytes for x in arrays), transcendentals=0
        ),
    )(*[pltpu.with_memory_space_constraint(x, pltpu.HBM) for x in arrays])


def decompress_kernel(
    lengths_hbm, weights_hbm, codes, residuals, centroids, rows_out, lengths, weights, table, sems
):
    passages, slots = codes.shape
    count, width = centroids.shape
    groups = count // GROUP
    small = [
        pltpu.make_async_copy(lengths_hbm, lengths, sems.at[0]),
        pltpu.make_async_copy(weights_hbm, weights, sems.at[1]),
    ]
    for copy in small:
        copy.start()
    for g in range(groups):
        table[:, g * width : (g + 1) * width] = centroids[g * GROUP : (g + 1) * GROUP, :]
    code_cols = jnp.swapaxes(codes[...].astype(jnp.float32), 0, 1).astype(jnp.int32)
    lane = lax.broadcasted_iota(jnp.int32, (slots, GROUP), 1)
    token = lax.broadcasted_iota(jnp.int32, (slots, width), 0)
    for first in range(0, passages, STEP):
        hot = []
        high = []
        for p in range(first, first + STEP):
            code = code_cols[:, p : p + 1]
            hot.append((lane == (code % GROUP)).astype(jnp.bfloat16))
            high.append(jnp.broadcast_to(code // GROUP, (slots, width)))
        spread = jnp.dot(
            jnp.concatenate(hot, 0), table[...], preferred_element_type=jnp.float32
        )
        if first == 0:
            for copy in small:
                copy.wait()
        for p in range(first, first + STEP):
            at = p - first
            part = spread[at * slots : (at + 1) * slots]
            cent = part[:, :width]
            for g in range(1, groups):
                cent = jnp.where(high[at] == g, part[:, g * width : (g + 1) * width], cent)
            code = residuals[p]
            odd = (code & 1) == 1
            low = jnp.where(odd, weights[1], weights[0])
            top = jnp.where(odd, weights[3], weights[2])
            values = cent + jnp.where(code >= 2, top, low)
            norm = lax.rsqrt(jnp.sum(values * values, axis=-1, keepdims=True) + 1e-06)
            exact = values * norm
            live = token < lengths[p]
            exact = jnp.where(live, exact, exact[0:1, :])
            cent = jnp.where(live, cent, cent[0:1, :])
            rows_out[p, :slots, :] = exact.astype(jnp.bfloat16)
            rows_out[p, slots:, :] = cent.astype(jnp.bfloat16)


def decompress(centroids, codes, residual_codes, lengths, bucket_weights):
    passages, slots = codes.shape
    count, width = centroids.shape
    scalars = [pltpu.with_memory_space_constraint(x, pltpu.HBM) for x in (lengths, bucket_weights)]
    arrays = [
        pltpu.with_memory_space_constraint(x, pltpu.VMEM)
        for x in (codes, residual_codes, centroids)
    ]
    return pl.pallas_call(
        decompress_kernel,
        in_specs=[pl.BlockSpec(memory_space=pltpu.HBM)] * 2
        + [pl.BlockSpec(memory_space=pltpu.VMEM)] * 3,
        out_specs=pl.BlockSpec(memory_space=pltpu.VMEM),
        out_shape=pltpu.VMEM((passages, 2 * slots, width), jnp.bfloat16),
        scratch_shapes=[
            pltpu.SMEM(lengths.shape, lengths.dtype),
            pltpu.SMEM(bucket_weights.shape, bucket_weights.dtype),
            pltpu.VMEM((GROUP, count // GROUP * width), jnp.bfloat16),
            pltpu.SemaphoreType.DMA((2,)),
        ],
        compiler_params=pltpu.CompilerParams(vmem_limit_bytes=44 * 2**20),
        cost_estimate=pl.CostEstimate(
            flops=2 * passages * slots * count * width,
            bytes_accessed=4 * passages * slots * width * 2,
            transcendentals=0,
        ),
    )(*scalars, *arrays)


def plan_kernel(shards, cap, passages, queries_hbm, candidates_hbm, block, plan, candidates, query_sem, cand_sem):
    q_local, top_k = candidates.shape
    tokens = queries_hbm.shape[0]
    send_queries = pltpu.make_async_copy(queries_hbm, block.at[pl.ds(0, tokens)], query_sem)
    get_candidates = pltpu.make_async_copy(candidates_hbm, candidates, cand_sem)
    get_candidates.start()
    send_queries.start()
    get_candidates.wait()
    slots = q_local * top_k
    per_row = shards // META
    cand = jnp.concatenate([candidates[q : q + 1, :] for q in range(q_local)], axis=1)
    target = cand // passages
    value = lax.broadcasted_iota(jnp.int32, (1, slots), 1) // top_k * passages + cand % passages + 1
    square = (slots, slots)
    wide = jnp.broadcast_to(target.astype(jnp.float32), square)
    earlier = lax.broadcasted_iota(jnp.int32, square, 0) < lax.broadcasted_iota(
        jnp.int32, square, 1
    )
    same = (jnp.swapaxes(wide, 0, 1) == wide) & earlier
    rank = jnp.sum(same.astype(jnp.int32), axis=0, keepdims=True)
    row = lax.broadcasted_iota(jnp.int32, (META, slots), 0)
    left = jnp.where(row == target // per_row, value.astype(jnp.float32), 0.0)
    lane = lax.broadcasted_iota(jnp.int32, (LANES, slots), 0)
    right = (lane == target % per_row * cap + rank).astype(jnp.float32)
    lists = lax.dot_general(
        left.astype(jnp.bfloat16),
        right.astype(jnp.bfloat16),
        (((1,), (1,)), ((), ())),
        preferred_element_type=jnp.float32,
    )
    block[tokens:, :] = lists.astype(jnp.bfloat16)
    plan[0:1, :] = target
    plan[1:2, :] = rank
    send_queries.wait()


def make_plan(queries, candidates, shards, cap, passages):
    tokens, width = queries.shape
    operands = (queries, candidates)
    return pl.pallas_call(
        functools.partial(plan_kernel, shards, cap, passages),
        in_specs=[pl.BlockSpec(memory_space=pltpu.HBM)] * 2,
        out_specs=[pl.BlockSpec(memory_space=pltpu.VMEM)] * 2,
        out_shape=(
            pltpu.VMEM((tokens + META, width), jnp.bfloat16),
            pltpu.VMEM((8, candidates.size), jnp.int32),
        ),
        scratch_shapes=[
            pltpu.VMEM(candidates.shape, candidates.dtype),
            pltpu.SemaphoreType.DMA,
            pltpu.SemaphoreType.DMA,
        ],
    )(*[pltpu.with_memory_space_constraint(x, pltpu.HBM) for x in operands])


def pieces(values):
    high = values.astype(jnp.bfloat16)
    rest = values - high.astype(jnp.float32)
    middle = rest.astype(jnp.bfloat16)
    low = (rest - middle.astype(jnp.float32)).astype(jnp.bfloat16)
    return [high, middle, low]


def exact_dot(values, mask, dims):
    rows = values.shape[0]
    parts = lax.dot_general(
        jnp.concatenate(pieces(values), axis=0),
        mask.astype(jnp.bfloat16),
        (dims, ((), ())),
        preferred_element_type=jnp.float32,
    )
    return parts[:rows] + parts[rows : 2 * rows] + parts[2 * rows :]


def score_kernel(query_tokens, cap, offsets, blocks, rows, out, listed, steps, tops, sem):
    passages, doubled, width = rows.shape
    slots = doubled // 2
    shards, block_rows, _ = blocks.shape
    per_row = shards // META
    me = lax.axis_index("shard")
    pairs = shards * cap
    max_steps = tops.shape[0] // 2
    bits = (passages - 1).bit_length()
    span = 1 << bits

    lists = blocks[:, block_rows - META :, :].reshape(shards * META, LANES)
    shape = (pairs, shards * META)
    pair = lax.broadcasted_iota(jnp.int32, shape, 0)
    wanted = pair // cap * META + me // per_row
    pick = (lax.broadcasted_iota(jnp.int32, shape, 1) == wanted).astype(jnp.bfloat16)
    found = jnp.dot(pick, lists, preferred_element_type=jnp.float32)
    shape = (pairs, LANES)
    lane = me % per_row * cap + lax.broadcasted_iota(jnp.int32, shape, 0) % cap
    own = lax.broadcasted_iota(jnp.int32, shape, 1) == lane
    column = jnp.sum(jnp.where(own, found, 0.0), axis=1, keepdims=True)
    wide = jnp.broadcast_to(column, shape)
    code_row = jnp.swapaxes(wide, 0, 1)[0:1, :].astype(jnp.int32)
    code_col = wide.astype(jnp.int32)

    def passage_of(code):
        return jnp.where(code > 0, (code - 1) % passages, passages)

    valid = code_row > 0
    p_row = passage_of(code_row)
    p_col = passage_of(code_col)[:, 0:1]
    square = (pairs, pairs)
    earlier = lax.broadcasted_iota(jnp.int32, square, 0) < lax.broadcasted_iota(
        jnp.int32, square, 1
    )
    rank = jnp.sum(((p_col == p_row) & earlier).astype(jnp.int32), axis=0, keepdims=True)
    shape = (passages, pairs)
    p_iota = lax.broadcasted_iota(jnp.int32, shape, 0)
    count = jnp.sum((p_iota == p_row).astype(jnp.int32), axis=1, keepdims=True)
    need = (count + PACK - 1) // PACK
    start = jnp.sum(jnp.where(p_iota < p_row, need, 0), axis=0, keepdims=True)
    step_row = jnp.where(valid, start + rank // PACK, max_steps)
    place_row = rank % PACK
    pair_row = lax.broadcasted_iota(jnp.int32, (1, pairs), 1)
    query_row = pair_row // cap * (block_rows // 16) + (code_row - 1) // passages * (
        query_tokens // 16
    )
    entry = jnp.where(valid, query_row * span + p_row, 0).astype(jnp.float32)
    in_step = lax.broadcasted_iota(jnp.int32, (LANES, pairs), 0) == step_row
    in_step = in_step.astype(jnp.float32)
    here = lax.broadcasted_iota(jnp.int32, (PACK, pairs), 0) == place_row
    entries = exact_dot(jnp.where(here, entry, 0.0), in_step, ((1,), (1,)))
    total = jnp.sum(need, axis=0, keepdims=True)
    lane = lax.broadcasted_iota(jnp.int32, (PACK, LANES), 1)
    listed[...] = jnp.where(lane == LANES - 1, total, entries.astype(jnp.int32))
    copy = pltpu.make_async_copy(listed, steps, sem)
    copy.start()
    tops[...] = jnp.zeros_like(tops)
    copy.wait()

    flat = blocks.reshape(shards * block_rows, width)

    def one_step(step):
        packed = [
            flat[pl.ds(pl.multiple_of((steps[k, step] >> bits) * 16, 16), query_tokens), :]
            for k in range(PACK)
        ]
        dots = lax.dot_general(
            rows[steps[0, step] & (span - 1)],
            jnp.concatenate(packed, axis=0),
            (((1,), (1,)), ((), ())),
            preferred_element_type=jnp.float32,
        )
        best = jnp.max(dots.reshape(2, slots, PACK * query_tokens), axis=1)
        tops[step : step + 1, :] = best[0:1]
        tops[max_steps + step : max_steps + step + 1, :] = best[1:2]

    taken = steps[0, LANES - 1]
    for begin, end in zip(CUTS, CUTS[1:] + (max_steps,)):

        @pl.when(taken > begin)
        def _():
            for step in range(begin, end):
                one_step(step)

    shape = (PACK, PACK * query_tokens)
    own = lax.broadcasted_iota(jnp.int32, shape, 1) // query_tokens
    own = (own == lax.broadcasted_iota(jnp.int32, shape, 0)).astype(jnp.float32)
    sums = exact_dot(tops[...], own, ((1,), (1,)))
    spread = [
        lax.dot_general(
            jnp.concatenate(pieces(sums[at * max_steps : (at + 1) * max_steps]), axis=1),
            in_step[:max_steps].astype(jnp.bfloat16),
            (((0,), (0,)), ((), ())),
            preferred_element_type=jnp.float32,
        )
        for at in range(2)
    ]
    exact = jnp.sum(jnp.where(here, spread[0][:PACK] + spread[0][PACK:2*PACK] + spread[0][2*PACK:], 0.0), axis=0, keepdims=True)
    approx = jnp.sum(jnp.where(here, spread[1][:PACK] + spread[1][PACK:2*PACK] + spread[1][2*PACK:], 0.0), axis=0, keepdims=True)
    shape = (shards, 2 * pairs)
    pair = lax.broadcasted_iota(jnp.int32, shape, 1)
    from_shard = pair % pairs // cap == lax.broadcasted_iota(jnp.int32, shape, 0)
    scores = jnp.where(from_shard, jnp.concatenate([exact, approx], axis=1), 0.0)
    shape = (LANES, 2 * pairs)
    pair = lax.broadcasted_iota(jnp.int32, shape, 1)
    lane = pair // pairs * (LANES // 2) + pair % cap
    to_lane = (lax.broadcasted_iota(jnp.int32, shape, 0) == lane).astype(jnp.float32)
    back = exact_dot(scores, to_lane, ((1,), (1,)))
    out[...] = jnp.zeros_like(out)
    for k, offset in enumerate(offsets):
        out[jnp.bitwise_xor(me, offset), 0:1, :] = back[k : k + 1, :]


def score(blocks, rows, offsets, query_tokens, cap):
    passages, doubled, width = rows.shape
    shards = len(offsets)
    max_steps = -(-(shards * cap + (PACK - 1) * passages) // (8 * PACK)) * 8
    return pl.pallas_call(
        functools.partial(score_kernel, query_tokens, cap, offsets),
        out_shape=jax.ShapeDtypeStruct((shards, 8, LANES), jnp.float32),
        scratch_shapes=[
            pltpu.VMEM((PACK, LANES), jnp.int32),
            pltpu.SMEM((PACK, LANES), jnp.int32),
            pltpu.VMEM((2 * max_steps, PACK * query_tokens), jnp.float32),
            pltpu.SemaphoreType.DMA,
        ],
        compiler_params=pltpu.CompilerParams(vmem_limit_bytes=48 * 2**20),
        cost_estimate=pl.CostEstimate(
            flops=2 * max_steps * PACK * query_tokens * doubled * width,
            bytes_accessed=2 * (blocks.size + rows.size),
            transcendentals=0,
        ),
    )(blocks, rows)


def pick_kernel(plan, scores, exact_out, approx_out):
    q_local, top_k = exact_out.shape
    shards, padded, lanes = scores.shape
    slots = q_local * top_k
    target = plan[0:1, :]
    rank = plan[1:2, :]
    source = lax.broadcasted_iota(jnp.int32, (shards * padded, slots), 0)
    hot = (source == target * padded).astype(jnp.bfloat16)
    values = scores[...].reshape(shards * padded, lanes)
    spread = sum(
        lax.dot_general(
            part, hot, (((0,), (0,)), ((), ())), preferred_element_type=jnp.float32
        )
        for part in pieces(values)
    )
    lane = lax.broadcasted_iota(jnp.int32, (lanes, slots), 0)
    exact = jnp.sum(jnp.where(lane == rank, spread, 0.0), axis=0, keepdims=True)
    approx = jnp.sum(jnp.where(lane == rank + lanes // 2, spread, 0.0), axis=0, keepdims=True)
    for q in range(q_local):
        exact_out[q : q + 1, :] = exact[:, q * top_k : (q + 1) * top_k]
        approx_out[q : q + 1, :] = approx[:, q * top_k : (q + 1) * top_k]


def pick(plan, scores, shape):
    result = jax.ShapeDtypeStruct(shape, jnp.float32)
    operands = [pltpu.with_memory_space_constraint(x, pltpu.VMEM) for x in (plan, scores)]
    return pl.pallas_call(pick_kernel, out_shape=(result, result))(*operands)


def exchange(block, steps, shards):
    others = [
        lax.ppermute(block, "shard", [(i, i ^ step) for i in range(shards)]) for step in steps
    ]
    return jnp.concatenate([block] + others, axis=0)


def per_device(queries, centroids, codes, residual_codes, lengths, bucket_weights, candidates):
    shards = lax.axis_size("shard")
    passages = codes.shape[0]
    q_local, query_tokens, width = queries.shape
    cap = max(2, 2 * candidates.size // shards)
    block, plan = make_plan(
        queries.reshape(q_local * query_tokens, width), candidates, shards, cap, passages
    )
    block_rows = block.shape[0]
    block, codes = lax.optimization_barrier((block, codes))
    codes, residual_codes, centroids = fetch(codes, residual_codes, centroids)
    offsets = [0]
    stride = shards
    while stride > 1:
        ways = 4 if stride % 4 == 0 else 2
        stride //= ways
        steps = [stride * k for k in range(1, ways)]
        block = exchange(block, steps, shards)
        offsets = [k ^ at for k in [0] + steps for at in offsets]
        if stride > 1:
            block, lengths = lax.optimization_barrier((block, lengths))
    rows = decompress(centroids, codes, residual_codes, lengths, bucket_weights)
    scores = score(block.reshape(shards, block_rows, width), rows, offsets, query_tokens, cap)
    back = lax.all_to_all(scores, "shard", split_axis=0, concat_axis=0, tiled=True)
    return pick(plan, back, candidates.shape)


def solution(mesh):
    placed = (
        P(("rep", "shard"), None, None),
        P("shard", None),
        P("shard", None),
        P("shard", None, None),
        P("shard"),
        P(),
        P(("rep", "shard"), None),
    )
    return jax.shard_map(
        per_device,
        mesh=mesh,
        in_specs=placed,
        out_specs=(P(("rep", "shard"), None), P(("rep", "shard"), None)),
        check_vma=False,
    )
```

```python
import functools

import jax
import jax.numpy as jnp
from jax import lax
from jax.experimental import pallas as pl
from jax.experimental.pallas import tpu as pltpu
from jax.sharding import PartitionSpec as P

GROUP = 256
STEP = 4
META = 16
LANES = 128
PACK = 8
CUTS = (0, 32, 48)


def fetch_kernel(
    lengths_hbm, codes_hbm, residuals_hbm, centroids_hbm,
    residuals, hot, high, table, lengths, codes, centroids, sems,
):
    passages, slots = codes.shape
    count, width = centroids.shape
    copies = [
        pltpu.make_async_copy(source, target, sems.at[i])
        for i, (source, target) in enumerate(
            (
                (lengths_hbm, lengths),
                (codes_hbm, codes),
                (centroids_hbm, centroids),
                (residuals_hbm, residuals),
            )
        )
    ]
    for copy in copies:
        copy.start()
    copies[0].wait()
    copies[1].wait()
    columns = jnp.swapaxes(codes[...].astype(jnp.float32), 0, 1).astype(jnp.int32)
    live = lax.broadcasted_iota(jnp.int32, columns.shape, 0) < lengths[...]
    columns = jnp.where(live, columns, columns[0:1, :])
    low = columns % GROUP
    top = columns // GROUP
    lane = lax.broadcasted_iota(jnp.int32, (slots, GROUP), 1)
    for p in range(passages):
        at = slice(p * slots, (p + 1) * slots)
        hot[at, :] = (lane == low[:, p : p + 1]).astype(jnp.bfloat16)
        high[at, :] = jnp.broadcast_to(top[:, p : p + 1], (slots, width))
    copies[2].wait()
    for g in range(count // GROUP):
        table[:, g * width : (g + 1) * width] = centroids[g * GROUP : (g + 1) * GROUP, :]
    copies[3].wait()


def fetch(lengths, codes, residual_codes, centroids):
    passages, slots = codes.shape
    count, width = centroids.shape
    operands = (lengths.reshape(1, passages), codes, residual_codes, centroids)
    return pl.pallas_call(
        fetch_kernel,
        in_specs=[pl.BlockSpec(memory_space=pltpu.HBM)] * len(operands),
        out_specs=[pl.BlockSpec(memory_space=pltpu.VMEM)] * 4,
        out_shape=(
            pltpu.VMEM(residual_codes.shape, residual_codes.dtype),
            pltpu.VMEM((passages * slots, GROUP), jnp.bfloat16),
            pltpu.VMEM((passages * slots, width), jnp.int32),
            pltpu.VMEM((GROUP, count // GROUP * width), jnp.bfloat16),
        ),
        scratch_shapes=[
            pltpu.VMEM((1, passages), lengths.dtype),
            pltpu.VMEM(codes.shape, codes.dtype),
            pltpu.VMEM(centroids.shape, centroids.dtype),
            pltpu.SemaphoreType.DMA((len(operands),)),
        ],
        compiler_params=pltpu.CompilerParams(vmem_limit_bytes=24 * 2**20),
        cost_estimate=pl.CostEstimate(
            flops=0, bytes_accessed=2 * residual_codes.nbytes, transcendentals=0
        ),
    )(*[pltpu.with_memory_space_constraint(x, pltpu.HBM) for x in operands])


def decompress_kernel(
    lengths_hbm, weights_hbm, residuals, hot, high, table, rows_out, lengths, weights, sems
):
    passages, slots, width = residuals.shape
    groups = table.shape[1] // width
    small = [
        pltpu.make_async_copy(lengths_hbm, lengths, sems.at[0]),
        pltpu.make_async_copy(weights_hbm, weights, sems.at[1]),
    ]
    for copy in small:
        copy.start()
    token = lax.broadcasted_iota(jnp.int32, (slots, width), 0)
    for first in range(0, passages, STEP):
        spread = jnp.dot(
            hot[first * slots : (first + STEP) * slots, :],
            table[...],
            preferred_element_type=jnp.float32,
        )
        if first == 0:
            for copy in small:
                copy.wait()
        for p in range(first, first + STEP):
            at = p - first
            part = spread[at * slots : (at + 1) * slots]
            choice = [part[:, g * width : (g + 1) * width] for g in range(groups)]
            group = high[p * slots : (p + 1) * slots, :]
            bit = 1
            while len(choice) > 1:
                odd = (group & bit) != 0
                choice = [
                    jnp.where(odd, choice[k + 1], choice[k]) for k in range(0, len(choice), 2)
                ]
                bit *= 2
            cent = choice[0]
            code = residuals[p]
            code = jnp.where(token < lengths[p], code, code[0:1, :])
            odd = (code & 1) == 1
            low = jnp.where(odd, weights[1], weights[0])
            top = jnp.where(odd, weights[3], weights[2])
            values = cent + jnp.where(code >= 2, top, low)
            norm = lax.rsqrt(jnp.sum(values * values, axis=-1, keepdims=True) + 1e-06)
            rows_out[p, :slots, :] = (values * norm).astype(jnp.bfloat16)
            rows_out[p, slots:, :] = cent.astype(jnp.bfloat16)


def decompress(lengths, bucket_weights, residual_codes, hot, high, table):
    passages, slots, width = residual_codes.shape
    scalars = [pltpu.with_memory_space_constraint(x, pltpu.HBM) for x in (lengths, bucket_weights)]
    arrays = [
        pltpu.with_memory_space_constraint(x, pltpu.VMEM)
        for x in (residual_codes, hot, high, table)
    ]
    return pl.pallas_call(
        decompress_kernel,
        in_specs=[pl.BlockSpec(memory_space=pltpu.HBM)] * 2
        + [pl.BlockSpec(memory_space=pltpu.VMEM)] * 4,
        out_specs=pl.BlockSpec(memory_space=pltpu.VMEM),
        out_shape=pltpu.VMEM((passages, 2 * slots, width), jnp.bfloat16),
        scratch_shapes=[
            pltpu.SMEM(lengths.shape, lengths.dtype),
            pltpu.SMEM(bucket_weights.shape, bucket_weights.dtype),
            pltpu.SemaphoreType.DMA((2,)),
        ],
        compiler_params=pltpu.CompilerParams(vmem_limit_bytes=40 * 2**20),
        cost_estimate=pl.CostEstimate(
            flops=2 * hot.size * table.shape[1],
            bytes_accessed=4 * passages * slots * width * 2,
            transcendentals=0,
        ),
    )(*scalars, *arrays)


def plan_kernel(shards, cap, passages, ways, queries_hbm, candidates_hbm, block, plan, candidates, query_sem, cand_sem):
    q_local, top_k = candidates.shape
    tokens = queries_hbm.shape[0]
    send_queries = pltpu.make_async_copy(queries_hbm, block.at[pl.ds(0, tokens)], query_sem)
    get_candidates = pltpu.make_async_copy(candidates_hbm, candidates, cand_sem)
    get_candidates.start()
    send_queries.start()
    get_candidates.wait()
    slots = q_local * top_k
    per_row = shards // META
    cand = jnp.concatenate([candidates[q : q + 1, :] for q in range(q_local)], axis=1)
    target = cand // passages
    value = lax.broadcasted_iota(jnp.int32, (1, slots), 1) // top_k * passages + cand % passages + 1
    square = (slots, slots)
    wide = jnp.broadcast_to(target.astype(jnp.float32), square)
    earlier = lax.broadcasted_iota(jnp.int32, square, 0) < lax.broadcasted_iota(
        jnp.int32, square, 1
    )
    same = (jnp.swapaxes(wide, 0, 1) == wide) & earlier
    rank = jnp.sum(same.astype(jnp.int32), axis=0, keepdims=True)
    row = lax.broadcasted_iota(jnp.int32, (META, slots), 0)
    left = jnp.where(row == target // per_row, value.astype(jnp.float32), 0.0)
    digit = lax.axis_index("shard") // (shards // ways)
    lane = lax.broadcasted_iota(jnp.int32, (LANES, slots), 0) - digit * (per_row * cap)
    right = (lane == target % per_row * cap + rank).astype(jnp.float32)
    lists = lax.dot_general(
        left.astype(jnp.bfloat16),
        right.astype(jnp.bfloat16),
        (((1,), (1,)), ((), ())),
        preferred_element_type=jnp.float32,
    )
    block[tokens:, :] = lists.astype(jnp.bfloat16)
    plan[0:1, :] = target
    plan[1:2, :] = rank
    send_queries.wait()


def make_plan(queries, candidates, shards, cap, passages, ways):
    tokens, width = queries.shape
    operands = (queries, candidates)
    return pl.pallas_call(
        functools.partial(plan_kernel, shards, cap, passages, ways),
        in_specs=[pl.BlockSpec(memory_space=pltpu.HBM)] * 2,
        out_specs=[pl.BlockSpec(memory_space=pltpu.VMEM)] * 2,
        out_shape=(
            pltpu.VMEM((tokens + META, width), jnp.bfloat16),
            pltpu.VMEM((8, candidates.size), jnp.int32),
        ),
        scratch_shapes=[
            pltpu.VMEM(candidates.shape, candidates.dtype),
            pltpu.SemaphoreType.DMA,
            pltpu.SemaphoreType.DMA,
        ],
    )(*[pltpu.with_memory_space_constraint(x, pltpu.HBM) for x in operands])


def pieces(values):
    high = values.astype(jnp.bfloat16)
    rest = values - high.astype(jnp.float32)
    middle = rest.astype(jnp.bfloat16)
    low = (rest - middle.astype(jnp.float32)).astype(jnp.bfloat16)
    return [high, middle, low]


def exact_dot(values, mask, dims):
    rows = values.shape[0]
    parts = lax.dot_general(
        jnp.concatenate(pieces(values), axis=0),
        mask.astype(jnp.bfloat16),
        (dims, ((), ())),
        preferred_element_type=jnp.float32,
    )
    return parts[:rows] + parts[rows : 2 * rows] + parts[2 * rows :]


def score_kernel(query_tokens, cap, ways, offsets, blocks, rows, out, listed, steps, tops, sem):
    passages, doubled, width = rows.shape
    slots = doubled // 2
    outer, block_rows, _ = blocks.shape
    shards = len(offsets)
    shard_rows = (block_rows - META) // ways
    per_row = shards // META
    me = lax.axis_index("shard")
    pairs = shards * cap
    max_steps = tops.shape[0] // 2
    bits = (passages - 1).bit_length()
    span = 1 << bits

    lists = blocks[:, block_rows - META :, :].reshape(outer * META, LANES)
    shape = (pairs, outer * META)
    pair = lax.broadcasted_iota(jnp.int32, shape, 0)
    wanted = pair // (cap * ways) * META + me // per_row
    pick = (lax.broadcasted_iota(jnp.int32, shape, 1) == wanted).astype(jnp.bfloat16)
    found = jnp.dot(pick, lists, preferred_element_type=jnp.float32)
    shape = (pairs, LANES)
    pair = lax.broadcasted_iota(jnp.int32, shape, 0)
    digit = jnp.bitwise_xor(me // (shards // ways), (ways - pair // cap % ways) % ways)
    lane = (digit * per_row + me % per_row) * cap + pair % cap
    own = lax.broadcasted_iota(jnp.int32, shape, 1) == lane
    column = jnp.sum(jnp.where(own, found, 0.0), axis=1, keepdims=True)
    wide = jnp.broadcast_to(column, shape)
    code_row = jnp.swapaxes(wide, 0, 1)[0:1, :].astype(jnp.int32)
    code_col = wide.astype(jnp.int32)

    def passage_of(code):
        return jnp.where(code > 0, (code - 1) % passages, passages)

    valid = code_row > 0
    p_row = passage_of(code_row)
    p_col = passage_of(code_col)[:, 0:1]
    square = (pairs, pairs)
    earlier = lax.broadcasted_iota(jnp.int32, square, 0) < lax.broadcasted_iota(
        jnp.int32, square, 1
    )
    rank = jnp.sum(((p_col == p_row) & earlier).astype(jnp.int32), axis=0, keepdims=True)
    shape = (passages, pairs)
    p_iota = lax.broadcasted_iota(jnp.int32, shape, 0)
    count = jnp.sum((p_iota == p_row).astype(jnp.int32), axis=1, keepdims=True)
    need = (count + PACK - 1) // PACK
    start = jnp.sum(jnp.where(p_iota < p_row, need, 0), axis=0, keepdims=True)
    step_row = jnp.where(valid, start + rank // PACK, max_steps)
    place_row = rank % PACK
    pair_row = lax.broadcasted_iota(jnp.int32, (1, pairs), 1)
    query_row = (
        pair_row // (cap * ways) * (block_rows // 16)
        + pair_row // cap % ways * (shard_rows // 16)
        + (code_row - 1) // passages * (query_tokens // 16)
    )
    entry = jnp.where(valid, query_row * span + p_row, 0).astype(jnp.float32)
    in_step = lax.broadcasted_iota(jnp.int32, (LANES, pairs), 0) == step_row
    in_step = in_step.astype(jnp.float32)
    here = lax.broadcasted_iota(jnp.int32, (PACK, pairs), 0) == place_row
    entries = exact_dot(jnp.where(here, entry, 0.0), in_step, ((1,), (1,)))
    total = jnp.sum(need, axis=0, keepdims=True)
    lane = lax.broadcasted_iota(jnp.int32, (PACK, LANES), 1)
    listed[...] = jnp.where(lane == LANES - 1, total, entries.astype(jnp.int32))
    copy = pltpu.make_async_copy(listed, steps, sem)
    copy.start()
    tops[...] = jnp.zeros_like(tops)
    copy.wait()

    flat = blocks.reshape(outer * block_rows, width)

    def one_step(step):
        packed = [
            flat[pl.ds(pl.multiple_of((steps[k, step] >> bits) * 16, 16), query_tokens), :]
            for k in range(PACK)
        ]
        dots = lax.dot_general(
            rows[steps[0, step] & (span - 1)],
            jnp.concatenate(packed, axis=0),
            (((1,), (1,)), ((), ())),
            preferred_element_type=jnp.float32,
        )
        best = jnp.max(dots.reshape(2, slots, PACK * query_tokens), axis=1)
        tops[step : step + 1, :] = best[0:1]
        tops[max_steps + step : max_steps + step + 1, :] = best[1:2]

    taken = steps[0, LANES - 1]
    for begin, end in zip(CUTS, CUTS[1:] + (max_steps,)):

        @pl.when(taken > begin)
        def _():
            for step in range(begin, end):
                one_step(step)

    shape = (PACK, PACK * query_tokens)
    own = lax.broadcasted_iota(jnp.int32, shape, 1) // query_tokens
    own = (own == lax.broadcasted_iota(jnp.int32, shape, 0)).astype(jnp.float32)
    sums = exact_dot(tops[...], own, ((1,), (1,)))
    spread = [
        lax.dot_general(
            jnp.concatenate(pieces(sums[at * max_steps : (at + 1) * max_steps]), axis=1),
            in_step[:max_steps].astype(jnp.bfloat16),
            (((0,), (0,)), ((), ())),
            preferred_element_type=jnp.float32,
        )
        for at in range(2)
    ]
    exact = jnp.sum(jnp.where(here, spread[0][:PACK] + spread[0][PACK:2*PACK] + spread[0][2*PACK:], 0.0), axis=0, keepdims=True)
    approx = jnp.sum(jnp.where(here, spread[1][:PACK] + spread[1][PACK:2*PACK] + spread[1][2*PACK:], 0.0), axis=0, keepdims=True)
    shape = (shards, 2 * pairs)
    pair = lax.broadcasted_iota(jnp.int32, shape, 1)
    from_shard = pair % pairs // cap == lax.broadcasted_iota(jnp.int32, shape, 0)
    scores = jnp.where(from_shard, jnp.concatenate([exact, approx], axis=1), 0.0)
    shape = (LANES, 2 * pairs)
    pair = lax.broadcasted_iota(jnp.int32, shape, 1)
    lane = pair // pairs * (LANES // 2) + pair % cap
    to_lane = (lax.broadcasted_iota(jnp.int32, shape, 0) == lane).astype(jnp.float32)
    back = exact_dot(scores, to_lane, ((1,), (1,)))
    for k, offset in enumerate(offsets):
        out[jnp.bitwise_xor(me, offset)] = back[k : k + 1, :]


def score(blocks, rows, offsets, query_tokens, cap, ways):
    passages, doubled, width = rows.shape
    shards = len(offsets)
    max_steps = -(-(shards * cap + (PACK - 1) * passages) // (8 * PACK)) * 8
    return pl.pallas_call(
        functools.partial(score_kernel, query_tokens, cap, ways, offsets),
        out_shape=pltpu.VMEM((shards, 1, LANES), jnp.float32),
        scratch_shapes=[
            pltpu.VMEM((PACK, LANES), jnp.int32),
            pltpu.SMEM((PACK, LANES), jnp.int32),
            pltpu.VMEM((2 * max_steps, PACK * query_tokens), jnp.float32),
            pltpu.SemaphoreType.DMA,
        ],
        compiler_params=pltpu.CompilerParams(vmem_limit_bytes=48 * 2**20),
        cost_estimate=pl.CostEstimate(
            flops=2 * max_steps * PACK * query_tokens * doubled * width,
            bytes_accessed=2 * (blocks.size + rows.size),
            transcendentals=0,
        ),
    )(blocks, rows)


def pick_kernel(plan, scores, exact_out, approx_out):
    q_local, top_k = exact_out.shape
    shards, padded, lanes = scores.shape
    slots = q_local * top_k
    target = plan[0:1, :]
    rank = plan[1:2, :]
    source = lax.broadcasted_iota(jnp.int32, (shards * padded, slots), 0)
    hot = (source == target * padded).astype(jnp.bfloat16)
    values = scores[...].reshape(shards * padded, lanes)
    spread = sum(
        lax.dot_general(
            part, hot, (((0,), (0,)), ((), ())), preferred_element_type=jnp.float32
        )
        for part in pieces(values)
    )
    lane = lax.broadcasted_iota(jnp.int32, (lanes, slots), 0)
    exact = jnp.sum(jnp.where(lane == rank, spread, 0.0), axis=0, keepdims=True)
    approx = jnp.sum(jnp.where(lane == rank + lanes // 2, spread, 0.0), axis=0, keepdims=True)
    for q in range(q_local):
        exact_out[q : q + 1, :] = exact[:, q * top_k : (q + 1) * top_k]
        approx_out[q : q + 1, :] = approx[:, q * top_k : (q + 1) * top_k]


def pick(plan, scores, shape):
    result = jax.ShapeDtypeStruct(shape, jnp.float32)
    operands = [pltpu.with_memory_space_constraint(x, pltpu.VMEM) for x in (plan, scores)]
    return pl.pallas_call(pick_kernel, out_shape=(result, result))(*operands)


def exchange(block, steps, shards):
    others = [
        lax.ppermute(block, "shard", [(i, i ^ step) for i in range(shards)]) for step in steps
    ]
    return [block] + others


def per_device(queries, centroids, codes, residual_codes, lengths, bucket_weights, candidates):
    shards = lax.axis_size("shard")
    passages = codes.shape[0]
    q_local, query_tokens, width = queries.shape
    tokens = q_local * query_tokens
    cap = max(2, 2 * candidates.size // shards)
    first_ways = 4 if shards % 4 == 0 else 2
    block, plan = make_plan(
        queries.reshape(tokens, width), candidates, shards, cap, passages, first_ways
    )
    block, codes = lax.optimization_barrier((block, codes))
    residual_codes, hot, high, table = fetch(lengths, codes, residual_codes, centroids)
    offsets = [0]
    stride = shards
    while stride > 1:
        ways = 4 if stride % 4 == 0 else 2
        steps = [stride // ways * k for k in range(ways - 1, 0, -1)]
        blocks = exchange(block, steps, shards)
        if stride == shards:
            block = jnp.concatenate([x[:tokens] for x in blocks] + [sum(x[tokens:] for x in blocks)])
        else:
            block = jnp.concatenate(blocks)
        offsets = [k ^ at for k in [0] + steps for at in offsets]
        stride //= ways
        if stride > 1:
            block, lengths = lax.optimization_barrier((block, lengths))
    rows = decompress(lengths, bucket_weights, residual_codes, hot, high, table)
    blocks = block.reshape(shards // first_ways, first_ways * tokens + META, width)
    scores = score(blocks, rows, offsets, query_tokens, cap, first_ways)
    back = lax.all_to_all(scores, "shard", split_axis=0, concat_axis=0, tiled=True)
    return pick(plan, back, candidates.shape)


def solution(mesh):
    placed = (
        P(("rep", "shard"), None, None),
        P("shard", None),
        P("shard", None),
        P("shard", None, None),
        P("shard"),
        P(),
        P(("rep", "shard"), None),
    )
    return jax.shard_map(
        per_device,
        mesh=mesh,
        in_specs=placed,
        out_specs=(P(("rep", "shard"), None), P(("rep", "shard"), None)),
        check_vma=False,
    )
```

```python
import functools

import jax
import jax.numpy as jnp
from jax import lax
from jax.experimental import pallas as pl
from jax.experimental.pallas import tpu as pltpu
from jax.sharding import PartitionSpec as P

GROUP = 256
STEP = 4
META = 16
LANES = 128
PACK = 4
SIDES = 2
CUTS = (0, 24, 40)


def fetch_kernel(
    lengths_hbm, codes_hbm, residuals_hbm, centroids_hbm,
    residuals, hot, high, table, lengths, codes, centroids, sems,
):
    passages, slots = codes.shape
    count, width = centroids.shape
    copies = [
        pltpu.make_async_copy(source, target, sems.at[i])
        for i, (source, target) in enumerate(
            (
                (lengths_hbm, lengths),
                (codes_hbm, codes),
                (centroids_hbm, centroids),
                (residuals_hbm, residuals),
            )
        )
    ]
    for copy in copies:
        copy.start()
    copies[0].wait()
    copies[1].wait()
    columns = jnp.swapaxes(codes[...].astype(jnp.float32), 0, 1).astype(jnp.int32)
    live = lax.broadcasted_iota(jnp.int32, columns.shape, 0) < lengths[...]
    columns = jnp.where(live, columns, columns[0:1, :])
    low = columns % GROUP
    top = columns // GROUP
    lane = lax.broadcasted_iota(jnp.int32, (slots, GROUP), 1)
    for p in range(passages):
        at = slice(p * slots, (p + 1) * slots)
        hot[at, :] = (lane == low[:, p : p + 1]).astype(jnp.bfloat16)
        high[at, :] = jnp.broadcast_to(top[:, p : p + 1], (slots, width))
    copies[2].wait()
    for g in range(count // GROUP):
        table[:, g * width : (g + 1) * width] = centroids[g * GROUP : (g + 1) * GROUP, :]
    copies[3].wait()


def fetch(lengths, codes, residual_codes, centroids):
    passages, slots = codes.shape
    count, width = centroids.shape
    operands = (lengths.reshape(1, passages), codes, residual_codes, centroids)
    return pl.pallas_call(
        fetch_kernel,
        in_specs=[pl.BlockSpec(memory_space=pltpu.HBM)] * len(operands),
        out_specs=[pl.BlockSpec(memory_space=pltpu.VMEM)] * 4,
        out_shape=(
            pltpu.VMEM(residual_codes.shape, residual_codes.dtype),
            pltpu.VMEM((passages * slots, GROUP), jnp.bfloat16),
            pltpu.VMEM((passages * slots, width), jnp.int32),
            pltpu.VMEM((GROUP, count // GROUP * width), jnp.bfloat16),
        ),
        scratch_shapes=[
            pltpu.VMEM((1, passages), lengths.dtype),
            pltpu.VMEM(codes.shape, codes.dtype),
            pltpu.VMEM(centroids.shape, centroids.dtype),
            pltpu.SemaphoreType.DMA((len(operands),)),
        ],
        compiler_params=pltpu.CompilerParams(vmem_limit_bytes=24 * 2**20),
        cost_estimate=pl.CostEstimate(
            flops=0, bytes_accessed=2 * residual_codes.nbytes, transcendentals=0
        ),
    )(*[pltpu.with_memory_space_constraint(x, pltpu.HBM) for x in operands])


def decompress_kernel(
    lengths_hbm, weights_hbm, residuals, hot, high, table, rows_out, lengths, weights, sems
):
    passages, slots, width = residuals.shape
    groups = table.shape[1] // width
    small = [
        pltpu.make_async_copy(lengths_hbm, lengths, sems.at[0]),
        pltpu.make_async_copy(weights_hbm, weights, sems.at[1]),
    ]
    for copy in small:
        copy.start()
    token = lax.broadcasted_iota(jnp.int32, (slots, width), 0)
    for first in range(0, passages, STEP):
        spread = jnp.dot(
            hot[first * slots : (first + STEP) * slots, :],
            table[...],
            preferred_element_type=jnp.float32,
        )
        if first == 0:
            for copy in small:
                copy.wait()
        for p in range(first, first + STEP):
            at = p - first
            part = spread[at * slots : (at + 1) * slots]
            choice = [part[:, g * width : (g + 1) * width] for g in range(groups)]
            group = high[p * slots : (p + 1) * slots, :]
            bit = 1
            while len(choice) > 1:
                odd = (group & bit) != 0
                choice = [
                    jnp.where(odd, choice[k + 1], choice[k]) for k in range(0, len(choice), 2)
                ]
                bit *= 2
            cent = choice[0]
            code = residuals[p]
            code = jnp.where(token < lengths[p], code, code[0:1, :])
            odd = (code & 1) == 1
            low = jnp.where(odd, weights[1], weights[0])
            top = jnp.where(odd, weights[3], weights[2])
            values = cent + jnp.where(code >= 2, top, low)
            norm = lax.rsqrt(jnp.sum(values * values, axis=-1, keepdims=True) + 1e-06)
            rows_out[p, :slots, :] = (values * norm).astype(jnp.bfloat16)
            rows_out[p, slots:, :] = cent.astype(jnp.bfloat16)


def decompress(lengths, bucket_weights, residual_codes, hot, high, table):
    passages, slots, width = residual_codes.shape
    scalars = [pltpu.with_memory_space_constraint(x, pltpu.HBM) for x in (lengths, bucket_weights)]
    arrays = [
        pltpu.with_memory_space_constraint(x, pltpu.VMEM)
        for x in (residual_codes, hot, high, table)
    ]
    return pl.pallas_call(
        decompress_kernel,
        in_specs=[pl.BlockSpec(memory_space=pltpu.HBM)] * 2
        + [pl.BlockSpec(memory_space=pltpu.VMEM)] * 4,
        out_specs=pl.BlockSpec(memory_space=pltpu.VMEM),
        out_shape=pltpu.VMEM((passages, 2 * slots, width), jnp.bfloat16),
        scratch_shapes=[
            pltpu.SMEM(lengths.shape, lengths.dtype),
            pltpu.SMEM(bucket_weights.shape, bucket_weights.dtype),
            pltpu.SemaphoreType.DMA((2,)),
        ],
        compiler_params=pltpu.CompilerParams(vmem_limit_bytes=40 * 2**20),
        cost_estimate=pl.CostEstimate(
            flops=2 * hot.size * table.shape[1],
            bytes_accessed=4 * passages * slots * width * 2,
            transcendentals=0,
        ),
    )(*scalars, *arrays)


def plan_kernel(shards, cap, passages, ways, queries_hbm, candidates_hbm, block, plan, candidates, query_sem, cand_sem):
    q_local, top_k = candidates.shape
    tokens = queries_hbm.shape[0]
    send_queries = pltpu.make_async_copy(queries_hbm, block.at[pl.ds(0, tokens)], query_sem)
    get_candidates = pltpu.make_async_copy(candidates_hbm, candidates, cand_sem)
    get_candidates.start()
    send_queries.start()
    get_candidates.wait()
    slots = q_local * top_k
    per_row = shards // META
    cand = jnp.concatenate([candidates[q : q + 1, :] for q in range(q_local)], axis=1)
    target = cand // passages
    value = lax.broadcasted_iota(jnp.int32, (1, slots), 1) // top_k * passages + cand % passages + 1
    square = (slots, slots)
    wide = jnp.broadcast_to(target.astype(jnp.float32), square)
    earlier = lax.broadcasted_iota(jnp.int32, square, 0) < lax.broadcasted_iota(
        jnp.int32, square, 1
    )
    same = (jnp.swapaxes(wide, 0, 1) == wide) & earlier
    rank = jnp.sum(same.astype(jnp.int32), axis=0, keepdims=True)
    row = lax.broadcasted_iota(jnp.int32, (META, slots), 0)
    left = jnp.where(row == target // per_row, value.astype(jnp.float32), 0.0)
    digit = lax.axis_index("shard") // (shards // ways)
    lane = lax.broadcasted_iota(jnp.int32, (LANES, slots), 0) - digit * (per_row * cap)
    right = (lane == target % per_row * cap + rank).astype(jnp.float32)
    lists = lax.dot_general(
        left.astype(jnp.bfloat16),
        right.astype(jnp.bfloat16),
        (((1,), (1,)), ((), ())),
        preferred_element_type=jnp.float32,
    )
    block[tokens:, :] = lists.astype(jnp.bfloat16)
    plan[0:1, :] = target
    plan[1:2, :] = rank
    send_queries.wait()


def make_plan(queries, candidates, shards, cap, passages, ways):
    tokens, width = queries.shape
    operands = (queries, candidates)
    return pl.pallas_call(
        functools.partial(plan_kernel, shards, cap, passages, ways),
        in_specs=[pl.BlockSpec(memory_space=pltpu.HBM)] * 2,
        out_specs=[pl.BlockSpec(memory_space=pltpu.VMEM)] * 2,
        out_shape=(
            pltpu.VMEM((tokens + META, width), jnp.bfloat16),
            pltpu.VMEM((8, candidates.size), jnp.int32),
        ),
        scratch_shapes=[
            pltpu.VMEM(candidates.shape, candidates.dtype),
            pltpu.SemaphoreType.DMA,
            pltpu.SemaphoreType.DMA,
        ],
    )(*[pltpu.with_memory_space_constraint(x, pltpu.HBM) for x in operands])


def pieces(values):
    high = values.astype(jnp.bfloat16)
    rest = values - high.astype(jnp.float32)
    middle = rest.astype(jnp.bfloat16)
    low = (rest - middle.astype(jnp.float32)).astype(jnp.bfloat16)
    return [high, middle, low]


def exact_dot(values, mask, dims):
    rows = values.shape[0]
    parts = lax.dot_general(
        jnp.concatenate(pieces(values), axis=0),
        mask.astype(jnp.bfloat16),
        (dims, ((), ())),
        preferred_element_type=jnp.float32,
    )
    return parts[:rows] + parts[rows : 2 * rows] + parts[2 * rows :]


def score_kernel(query_tokens, cap, ways, offsets, blocks, rows, out, listed, steps, tops, sem):
    passages, doubled, width = rows.shape
    slots = doubled // 2
    outer, block_rows, _ = blocks.shape
    shards = len(offsets)
    shard_rows = (block_rows - META) // ways
    per_row = shards // META
    me = lax.axis_index("shard")
    pairs = shards * cap
    max_steps = tops.shape[0] // 2
    bits = (passages - 1).bit_length()
    span = 1 << bits

    lists = blocks[:, block_rows - META :, :].reshape(outer * META, LANES)
    shape = (pairs, outer * META)
    pair = lax.broadcasted_iota(jnp.int32, shape, 0)
    wanted = pair // (cap * ways) * META + me // per_row
    pick = (lax.broadcasted_iota(jnp.int32, shape, 1) == wanted).astype(jnp.bfloat16)
    found = jnp.dot(pick, lists, preferred_element_type=jnp.float32)
    shape = (pairs, LANES)
    pair = lax.broadcasted_iota(jnp.int32, shape, 0)
    digit = jnp.bitwise_xor(me // (shards // ways), (ways - pair // cap % ways) % ways)
    lane = (digit * per_row + me % per_row) * cap + pair % cap
    own = lax.broadcasted_iota(jnp.int32, shape, 1) == lane
    column = jnp.sum(jnp.where(own, found, 0.0), axis=1, keepdims=True)
    wide = jnp.broadcast_to(column, shape)
    code_row = jnp.swapaxes(wide, 0, 1)[0:1, :].astype(jnp.int32)
    code_col = wide.astype(jnp.int32)

    def passage_of(code):
        return jnp.where(code > 0, (code - 1) % passages, passages)

    valid = code_row > 0
    p_row = passage_of(code_row)
    p_col = passage_of(code_col)[:, 0:1]
    square = (pairs, pairs)
    earlier = lax.broadcasted_iota(jnp.int32, square, 0) < lax.broadcasted_iota(
        jnp.int32, square, 1
    )
    rank = jnp.sum(((p_col == p_row) & earlier).astype(jnp.int32), axis=0, keepdims=True)
    shape = (passages, pairs)
    p_iota = lax.broadcasted_iota(jnp.int32, shape, 0)
    count = jnp.sum((p_iota == p_row).astype(jnp.int32), axis=1, keepdims=True)
    need = (count + PACK - 1) // PACK
    start = jnp.sum(jnp.where(p_iota < p_row, need, 0), axis=0, keepdims=True)
    half = start + rank // PACK
    step_row = jnp.where(valid, half // SIDES, max_steps)
    place_row = half % SIDES * PACK + rank % PACK
    pair_row = lax.broadcasted_iota(jnp.int32, (1, pairs), 1)
    query_row = (
        pair_row // (cap * ways) * (block_rows // 16)
        + pair_row // cap % ways * (shard_rows // 16)
        + (code_row - 1) // passages * (query_tokens // 16)
    )
    entry = jnp.where(valid, query_row * span + p_row, 0).astype(jnp.float32)
    in_step = lax.broadcasted_iota(jnp.int32, (LANES, pairs), 0) == step_row
    in_step = in_step.astype(jnp.float32)
    places = SIDES * PACK
    here = lax.broadcasted_iota(jnp.int32, (places, pairs), 0) == place_row
    entries = exact_dot(jnp.where(here, entry, 0.0), in_step, ((1,), (1,)))
    total = jnp.sum(need, axis=0, keepdims=True)
    lane = lax.broadcasted_iota(jnp.int32, (places, LANES), 1)
    total = (total + SIDES - 1) // SIDES
    listed[...] = jnp.where(lane == LANES - 1, total, entries.astype(jnp.int32))
    copy = pltpu.make_async_copy(listed, steps, sem)
    copy.start()
    tops[...] = jnp.zeros_like(tops)
    copy.wait()

    flat = blocks.reshape(outer * block_rows, width)

    blank = jnp.zeros((PACK * query_tokens, width), jnp.bfloat16)

    def one_step(step):
        sides = []
        packed = []
        for side in range(SIDES):
            first = side * PACK
            sides.append(rows[steps[first, step] & (span - 1)])
            queries = jnp.concatenate(
                [
                    flat[pl.ds(pl.multiple_of((steps[k, step] >> bits) * 16, 16), query_tokens), :]
                    for k in range(first, first + PACK)
                ],
                axis=0,
            )
            packed.append(
                jnp.concatenate([queries if at == side else blank for at in range(SIDES)], axis=1)
            )
        dots = lax.dot_general(
            jnp.concatenate(sides, axis=1),
            jnp.concatenate(packed, axis=0),
            (((1,), (1,)), ((), ())),
            preferred_element_type=jnp.float32,
        )
        best = jnp.max(dots.reshape(2, slots, places * query_tokens), axis=1)
        tops[step : step + 1, :] = best[0:1]
        tops[max_steps + step : max_steps + step + 1, :] = best[1:2]

    taken = steps[0, LANES - 1]
    for begin, end in zip(CUTS, CUTS[1:] + (max_steps,)):

        @pl.when(taken > begin)
        def _():
            for step in range(begin, end):
                one_step(step)

    shape = (places, places * query_tokens)
    own = lax.broadcasted_iota(jnp.int32, shape, 1) // query_tokens
    own = (own == lax.broadcasted_iota(jnp.int32, shape, 0)).astype(jnp.float32)
    parts = lax.dot_general(
        own.astype(jnp.bfloat16),
        jnp.concatenate(pieces(tops[...]), axis=0),
        (((1,), (1,)), ((), ())),
        preferred_element_type=jnp.float32,
    )
    rows_of = 2 * max_steps
    sums = parts[:, :rows_of] + parts[:, rows_of : 2 * rows_of] + parts[:, 2 * rows_of :]
    by_step = in_step[:max_steps]
    spread = [
        exact_dot(sums[:, at * max_steps : (at + 1) * max_steps], by_step, ((1,), (0,)))
        for at in range(2)
    ]
    exact = jnp.sum(jnp.where(here, spread[0], 0.0), axis=0, keepdims=True)
    approx = jnp.sum(jnp.where(here, spread[1], 0.0), axis=0, keepdims=True)
    shape = (shards, 2 * pairs)
    pair = lax.broadcasted_iota(jnp.int32, shape, 1)
    from_shard = pair % pairs // cap == lax.broadcasted_iota(jnp.int32, shape, 0)
    scores = jnp.where(from_shard, jnp.concatenate([exact, approx], axis=1), 0.0)
    shape = (LANES, 2 * pairs)
    pair = lax.broadcasted_iota(jnp.int32, shape, 1)
    lane = pair // pairs * (LANES // 2) + pair % cap
    to_lane = (lax.broadcasted_iota(jnp.int32, shape, 0) == lane).astype(jnp.float32)
    back = exact_dot(scores, to_lane, ((1,), (1,)))
    for k, offset in enumerate(offsets):
        out[jnp.bitwise_xor(me, offset)] = back[k : k + 1, :]


def score(blocks, rows, offsets, query_tokens, cap, ways):
    passages, doubled, width = rows.shape
    shards = len(offsets)
    places = SIDES * PACK
    max_steps = -(-(shards * cap + (PACK - 1) * passages) // (8 * places)) * 8
    return pl.pallas_call(
        functools.partial(score_kernel, query_tokens, cap, ways, offsets),
        out_shape=pltpu.VMEM((shards, 1, LANES), jnp.float32),
        scratch_shapes=[
            pltpu.VMEM((places, LANES), jnp.int32),
            pltpu.SMEM((places, LANES), jnp.int32),
            pltpu.VMEM((2 * max_steps, places * query_tokens), jnp.float32),
            pltpu.SemaphoreType.DMA,
        ],
        compiler_params=pltpu.CompilerParams(vmem_limit_bytes=48 * 2**20),
        cost_estimate=pl.CostEstimate(
            flops=2 * max_steps * places * query_tokens * doubled * width,
            bytes_accessed=2 * (blocks.size + rows.size),
            transcendentals=0,
        ),
    )(blocks, rows)


def pick_kernel(plan, scores, exact_out, approx_out):
    q_local, top_k = exact_out.shape
    shards, padded, lanes = scores.shape
    slots = q_local * top_k
    target = plan[0:1, :]
    rank = plan[1:2, :]
    source = lax.broadcasted_iota(jnp.int32, (shards * padded, slots), 0)
    hot = (source == target * padded).astype(jnp.bfloat16)
    values = scores[...].reshape(shards * padded, lanes)
    spread = sum(
        lax.dot_general(
            part, hot, (((0,), (0,)), ((), ())), preferred_element_type=jnp.float32
        )
        for part in pieces(values)
    )
    lane = lax.broadcasted_iota(jnp.int32, (lanes, slots), 0)
    exact = jnp.sum(jnp.where(lane == rank, spread, 0.0), axis=0, keepdims=True)
    approx = jnp.sum(jnp.where(lane == rank + lanes // 2, spread, 0.0), axis=0, keepdims=True)
    for q in range(q_local):
        exact_out[q : q + 1, :] = exact[:, q * top_k : (q + 1) * top_k]
        approx_out[q : q + 1, :] = approx[:, q * top_k : (q + 1) * top_k]


def pick(plan, scores, shape):
    result = jax.ShapeDtypeStruct(shape, jnp.float32)
    operands = [pltpu.with_memory_space_constraint(x, pltpu.VMEM) for x in (plan, scores)]
    return pl.pallas_call(pick_kernel, out_shape=(result, result))(*operands)


def exchange(block, steps, shards):
    others = [
        lax.ppermute(block, "shard", [(i, i ^ step) for i in range(shards)]) for step in steps
    ]
    return [block] + others


def per_device(queries, centroids, codes, residual_codes, lengths, bucket_weights, candidates):
    shards = lax.axis_size("shard")
    passages = codes.shape[0]
    q_local, query_tokens, width = queries.shape
    tokens = q_local * query_tokens
    cap = max(2, 2 * candidates.size // shards)
    first_ways = 4 if shards % 4 == 0 else 2
    block, plan = make_plan(
        queries.reshape(tokens, width), candidates, shards, cap, passages, first_ways
    )
    block, codes = lax.optimization_barrier((block, codes))
    residual_codes, hot, high, table = fetch(lengths, codes, residual_codes, centroids)
    offsets = [0]
    stride = shards
    while stride > 1:
        ways = 4 if stride % 4 == 0 else 2
        steps = [stride // ways * k for k in range(ways - 1, 0, -1)]
        blocks = exchange(block, steps, shards)
        if stride == shards:
            block = jnp.concatenate([x[:tokens] for x in blocks] + [sum(x[tokens:] for x in blocks)])
        else:
            block = jnp.concatenate(blocks)
        offsets = [k ^ at for k in [0] + steps for at in offsets]
        stride //= ways
        if stride > 1:
            block, lengths = lax.optimization_barrier((block, lengths))
    rows = decompress(lengths, bucket_weights, residual_codes, hot, high, table)
    blocks = block.reshape(shards // first_ways, first_ways * tokens + META, width)
    scores = score(blocks, rows, offsets, query_tokens, cap, first_ways)
    back = lax.all_to_all(scores, "shard", split_axis=0, concat_axis=0, tiled=True)
    return pick(plan, back, candidates.shape)


def solution(mesh):
    placed = (
        P(("rep", "shard"), None, None),
        P("shard", None),
        P("shard", None),
        P("shard", None, None),
        P("shard"),
        P(),
        P(("rep", "shard"), None),
    )
    return jax.shard_map(
        per_device,
        mesh=mesh,
        in_specs=placed,
        out_specs=(P(("rep", "shard"), None), P(("rep", "shard"), None)),
        check_vma=False,
    )
```

```python
import functools

import jax
import jax.numpy as jnp
from jax import lax
from jax.experimental import pallas as pl
from jax.experimental.pallas import tpu as pltpu
from jax.sharding import PartitionSpec as P

GROUP = 256
STEP = 4
META = 16
LANES = 128
PACK = 4
SIDES = 2
CUTS = (0, 24, 40)


def start_copies(sources, targets, sems):
    copies = [
        pltpu.make_async_copy(source, target, sems.at[i])
        for i, (source, target) in enumerate(zip(sources, targets))
    ]
    for copy in copies:
        copy.start()
    return copies


def prepare(copies, lengths_row, codes, centroids, hot, high, table):
    passages, slots = codes.shape
    count, width = centroids.shape
    copies[0].wait()
    copies[1].wait()
    columns = jnp.swapaxes(codes[...].astype(jnp.float32), 0, 1).astype(jnp.int32)
    live = lax.broadcasted_iota(jnp.int32, columns.shape, 0) < lengths_row[...]
    columns = jnp.where(live, columns, columns[0:1, :])
    low = columns % GROUP
    top = columns // GROUP
    lane = lax.broadcasted_iota(jnp.int32, (slots, GROUP), 1)
    for p in range(passages):
        at = slice(p * slots, (p + 1) * slots)
        hot[at, :] = (lane == low[:, p : p + 1]).astype(jnp.bfloat16)
        high[at, :] = jnp.broadcast_to(top[:, p : p + 1], (slots, width))
    copies[2].wait()
    for g in range(count // GROUP):
        table[:, g * width : (g + 1) * width] = centroids[g * GROUP : (g + 1) * GROUP, :]
    for copy in copies[3:]:
        copy.wait()


def build_rows(first, residuals, hot, high, table, rows, lengths, weights):
    _, slots, width = residuals.shape
    groups = table.shape[1] // width
    token = lax.broadcasted_iota(jnp.int32, (slots, width), 0)
    spread = jnp.dot(
        hot[first * slots : (first + STEP) * slots, :],
        table[...],
        preferred_element_type=jnp.float32,
    )
    for p in range(first, first + STEP):
        at = p - first
        part = spread[at * slots : (at + 1) * slots]
        choice = [part[:, g * width : (g + 1) * width] for g in range(groups)]
        group = high[p * slots : (p + 1) * slots, :]
        bit = 1
        while len(choice) > 1:
            odd = (group & bit) != 0
            choice = [jnp.where(odd, choice[k + 1], choice[k]) for k in range(0, len(choice), 2)]
            bit *= 2
        cent = choice[0]
        code = residuals[p]
        code = jnp.where(token < lengths[p], code, code[0:1, :])
        odd = (code & 1) == 1
        low = jnp.where(odd, weights[1], weights[0])
        top = jnp.where(odd, weights[3], weights[2])
        values = cent + jnp.where(code >= 2, top, low)
        norm = lax.rsqrt(jnp.sum(values * values, axis=-1, keepdims=True) + 1e-06)
        rows[p, :slots, :] = (values * norm).astype(jnp.bfloat16)
        rows[p, slots:, :] = cent.astype(jnp.bfloat16)


def fetches_late(ways):
    shards = lax.axis_size("shard")
    odd_member = lax.axis_index("shard") // (shards // ways) % 2 == 1
    return jnp.logical_and(odd_member, lax.axis_index("rep") % 2 == 1)


def fetch_kernel(ways, *refs):
    sources = refs[:6]
    residuals, hot, high, table = refs[6:10]
    lengths_row, codes, centroids, lengths, weights, sems = refs[10:]

    @pl.when(jnp.logical_not(fetches_late(ways)))
    def _():
        targets = (lengths_row, codes, centroids, lengths, weights, residuals)
        copies = start_copies(sources, targets, sems)
        prepare(copies, lengths_row, codes, centroids, hot, high, table)


def index_scratch(lengths, bucket_weights, codes, centroids, count):
    return [
        pltpu.VMEM((1, lengths.shape[0]), lengths.dtype),
        pltpu.VMEM(codes.shape, codes.dtype),
        pltpu.VMEM(centroids.shape, centroids.dtype),
        pltpu.SMEM(lengths.shape, lengths.dtype),
        pltpu.SMEM(bucket_weights.shape, bucket_weights.dtype),
        pltpu.SemaphoreType.DMA((count,)),
    ]


def index_arrays(codes, centroids, width):
    tokens = codes.size
    return [
        pltpu.VMEM(codes.shape + (width,), jnp.int32),
        pltpu.VMEM((tokens, GROUP), jnp.bfloat16),
        pltpu.VMEM((tokens, width), jnp.int32),
        pltpu.VMEM((GROUP, centroids.size // GROUP), jnp.bfloat16),
    ]


def fetch(lengths, bucket_weights, codes, residual_codes, centroids, ways):
    passages = codes.shape[0]
    width = centroids.shape[1]
    operands = (
        lengths.reshape(1, passages), codes, centroids, lengths, bucket_weights, residual_codes
    )
    return pl.pallas_call(
        functools.partial(fetch_kernel, ways),
        in_specs=[pl.BlockSpec(memory_space=pltpu.HBM)] * len(operands),
        out_specs=[pl.BlockSpec(memory_space=pltpu.VMEM)] * 4,
        out_shape=index_arrays(codes, centroids, width),
        scratch_shapes=index_scratch(lengths, bucket_weights, codes, centroids, len(operands)),
        compiler_params=pltpu.CompilerParams(vmem_limit_bytes=32 * 2**20),
        cost_estimate=pl.CostEstimate(
            flops=0, bytes_accessed=2 * residual_codes.nbytes, transcendentals=0
        ),
    )(*[pltpu.with_memory_space_constraint(x, pltpu.HBM) for x in operands])


def decompress_kernel(ways, *refs):
    sources = refs[:6]
    early = refs[6:10]
    rows = refs[10]
    lengths_row, codes, centroids, lengths, weights, sems = refs[11:17]
    own = refs[17:]
    passages = codes.shape[0]
    late = fetches_late(ways)

    @pl.when(jnp.logical_not(late))
    def _():
        copies = start_copies(sources[3:5], (lengths, weights), sems)
        for copy in copies:
            copy.wait()
        for first in range(0, passages, STEP):
            build_rows(first, *early, rows, lengths, weights)

    @pl.when(late)
    def _():
        targets = (lengths_row, codes, centroids, lengths, weights, own[0])
        copies = start_copies(sources, targets, sems)
        prepare(copies, lengths_row, codes, centroids, *own[1:])
        for first in range(0, passages, STEP):
            build_rows(first, *own, rows, lengths, weights)


def decompress(lengths, bucket_weights, codes, residual_codes, centroids, ways, early):
    passages, slots = codes.shape
    width = centroids.shape[1]
    operands = (
        lengths.reshape(1, passages), codes, centroids, lengths, bucket_weights, residual_codes
    )
    return pl.pallas_call(
        functools.partial(decompress_kernel, ways),
        in_specs=[pl.BlockSpec(memory_space=pltpu.HBM)] * len(operands)
        + [pl.BlockSpec(memory_space=pltpu.VMEM)] * len(early),
        out_specs=pl.BlockSpec(memory_space=pltpu.VMEM),
        out_shape=pltpu.VMEM((passages, 2 * slots, width), jnp.bfloat16),
        scratch_shapes=index_scratch(lengths, bucket_weights, codes, centroids, len(operands))
        + index_arrays(codes, centroids, width),
        compiler_params=pltpu.CompilerParams(vmem_limit_bytes=40 * 2**20),
        cost_estimate=pl.CostEstimate(
            flops=2 * codes.size * centroids.size,
            bytes_accessed=4 * codes.size * width,
            transcendentals=0,
        ),
    )(
        *[pltpu.with_memory_space_constraint(x, pltpu.HBM) for x in operands],
        *[pltpu.with_memory_space_constraint(x, pltpu.VMEM) for x in early],
    )


def plan_kernel(shards, cap, passages, ways, queries_hbm, candidates_hbm, block, plan, candidates, query_sem, cand_sem):
    q_local, top_k = candidates.shape
    tokens = queries_hbm.shape[0]
    send_queries = pltpu.make_async_copy(queries_hbm, block.at[pl.ds(0, tokens)], query_sem)
    get_candidates = pltpu.make_async_copy(candidates_hbm, candidates, cand_sem)
    get_candidates.start()
    send_queries.start()
    get_candidates.wait()
    slots = q_local * top_k
    per_row = shards // META
    cand = jnp.concatenate([candidates[q : q + 1, :] for q in range(q_local)], axis=1)
    target = cand // passages
    value = lax.broadcasted_iota(jnp.int32, (1, slots), 1) // top_k * passages + cand % passages + 1
    square = (slots, slots)
    wide = jnp.broadcast_to(target.astype(jnp.float32), square)
    earlier = lax.broadcasted_iota(jnp.int32, square, 0) < lax.broadcasted_iota(
        jnp.int32, square, 1
    )
    same = (jnp.swapaxes(wide, 0, 1) == wide) & earlier
    rank = jnp.sum(same.astype(jnp.int32), axis=0, keepdims=True)
    row = lax.broadcasted_iota(jnp.int32, (META, slots), 0)
    left = jnp.where(row == target // per_row, value.astype(jnp.float32), 0.0)
    digit = lax.axis_index("shard") // (shards // ways)
    lane = lax.broadcasted_iota(jnp.int32, (LANES, slots), 0) - digit * (per_row * cap)
    right = (lane == target % per_row * cap + rank).astype(jnp.float32)
    lists = lax.dot_general(
        left.astype(jnp.bfloat16),
        right.astype(jnp.bfloat16),
        (((1,), (1,)), ((), ())),
        preferred_element_type=jnp.float32,
    )
    block[tokens:, :] = lists.astype(jnp.bfloat16)
    plan[0:1, :] = target
    plan[1:2, :] = rank
    send_queries.wait()


def make_plan(queries, candidates, shards, cap, passages, ways):
    tokens, width = queries.shape
    operands = (queries, candidates)
    return pl.pallas_call(
        functools.partial(plan_kernel, shards, cap, passages, ways),
        in_specs=[pl.BlockSpec(memory_space=pltpu.HBM)] * 2,
        out_specs=[pl.BlockSpec(memory_space=pltpu.VMEM)] * 2,
        out_shape=(
            pltpu.VMEM((tokens + META, width), jnp.bfloat16),
            pltpu.VMEM((8, candidates.size), jnp.int32),
        ),
        scratch_shapes=[
            pltpu.VMEM(candidates.shape, candidates.dtype),
            pltpu.SemaphoreType.DMA,
            pltpu.SemaphoreType.DMA,
        ],
    )(*[pltpu.with_memory_space_constraint(x, pltpu.HBM) for x in operands])


def pieces(values):
    high = values.astype(jnp.bfloat16)
    rest = values - high.astype(jnp.float32)
    middle = rest.astype(jnp.bfloat16)
    low = (rest - middle.astype(jnp.float32)).astype(jnp.bfloat16)
    return [high, middle, low]


def exact_dot(values, mask, dims):
    rows = values.shape[0]
    parts = lax.dot_general(
        jnp.concatenate(pieces(values), axis=0),
        mask.astype(jnp.bfloat16),
        (dims, ((), ())),
        preferred_element_type=jnp.float32,
    )
    return parts[:rows] + parts[rows : 2 * rows] + parts[2 * rows :]


def score_kernel(query_tokens, cap, ways, offsets, blocks, rows, out, listed, steps, tops, sem):
    passages, doubled, width = rows.shape
    slots = doubled // 2
    outer, block_rows, _ = blocks.shape
    shards = len(offsets)
    shard_rows = (block_rows - META) // ways
    per_row = shards // META
    me = lax.axis_index("shard")
    pairs = shards * cap
    max_steps = tops.shape[0] // 2
    bits = (passages - 1).bit_length()
    span = 1 << bits

    lists = blocks[:, block_rows - META :, :].reshape(outer * META, LANES)
    shape = (pairs, outer * META)
    pair = lax.broadcasted_iota(jnp.int32, shape, 0)
    wanted = pair // (cap * ways) * META + me // per_row
    pick = (lax.broadcasted_iota(jnp.int32, shape, 1) == wanted).astype(jnp.bfloat16)
    found = jnp.dot(pick, lists, preferred_element_type=jnp.float32)
    shape = (pairs, LANES)
    pair = lax.broadcasted_iota(jnp.int32, shape, 0)
    digit = jnp.bitwise_xor(me // (shards // ways), (ways - pair // cap % ways) % ways)
    lane = (digit * per_row + me % per_row) * cap + pair % cap
    own = lax.broadcasted_iota(jnp.int32, shape, 1) == lane
    column = jnp.sum(jnp.where(own, found, 0.0), axis=1, keepdims=True)
    wide = jnp.broadcast_to(column, shape)
    code_row = jnp.swapaxes(wide, 0, 1)[0:1, :].astype(jnp.int32)
    code_col = wide.astype(jnp.int32)

    def passage_of(code):
        return jnp.where(code > 0, (code - 1) % passages, passages)

    valid = code_row > 0
    p_row = passage_of(code_row)
    p_col = passage_of(code_col)[:, 0:1]
    square = (pairs, pairs)
    earlier = lax.broadcasted_iota(jnp.int32, square, 0) < lax.broadcasted_iota(
        jnp.int32, square, 1
    )
    rank = jnp.sum(((p_col == p_row) & earlier).astype(jnp.int32), axis=0, keepdims=True)
    shape = (passages, pairs)
    p_iota = lax.broadcasted_iota(jnp.int32, shape, 0)
    count = jnp.sum((p_iota == p_row).astype(jnp.int32), axis=1, keepdims=True)
    need = (count + PACK - 1) // PACK
    start = jnp.sum(jnp.where(p_iota < p_row, need, 0), axis=0, keepdims=True)
    half = start + rank // PACK
    step_row = jnp.where(valid, half // SIDES, max_steps)
    place_row = half % SIDES * PACK + rank % PACK
    pair_row = lax.broadcasted_iota(jnp.int32, (1, pairs), 1)
    query_row = (
        pair_row // (cap * ways) * (block_rows // 16)
        + pair_row // cap % ways * (shard_rows // 16)
        + (code_row - 1) // passages * (query_tokens // 16)
    )
    entry = jnp.where(valid, query_row * span + p_row, 0).astype(jnp.float32)
    in_step = lax.broadcasted_iota(jnp.int32, (LANES, pairs), 0) == step_row
    in_step = in_step.astype(jnp.float32)
    places = SIDES * PACK
    here = lax.broadcasted_iota(jnp.int32, (places, pairs), 0) == place_row
    entries = exact_dot(jnp.where(here, entry, 0.0), in_step, ((1,), (1,)))
    total = jnp.sum(need, axis=0, keepdims=True)
    lane = lax.broadcasted_iota(jnp.int32, (places, LANES), 1)
    total = (total + SIDES - 1) // SIDES
    listed[...] = jnp.where(lane == LANES - 1, total, entries.astype(jnp.int32))
    copy = pltpu.make_async_copy(listed, steps, sem)
    copy.start()
    tops[...] = jnp.zeros_like(tops)
    copy.wait()

    flat = blocks.reshape(outer * block_rows, width)

    blank = jnp.zeros((PACK * query_tokens, width), jnp.bfloat16)

    def one_step(step):
        sides = []
        packed = []
        for side in range(SIDES):
            first = side * PACK
            sides.append(rows[steps[first, step] & (span - 1)])
            queries = jnp.concatenate(
                [
                    flat[pl.ds(pl.multiple_of((steps[k, step] >> bits) * 16, 16), query_tokens), :]
                    for k in range(first, first + PACK)
                ],
                axis=0,
            )
            packed.append(
                jnp.concatenate([queries if at == side else blank for at in range(SIDES)], axis=1)
            )
        dots = lax.dot_general(
            jnp.concatenate(sides, axis=1),
            jnp.concatenate(packed, axis=0),
            (((1,), (1,)), ((), ())),
            preferred_element_type=jnp.float32,
        )
        best = jnp.max(dots.reshape(2, slots, places * query_tokens), axis=1)
        tops[step : step + 1, :] = best[0:1]
        tops[max_steps + step : max_steps + step + 1, :] = best[1:2]

    taken = steps[0, LANES - 1]
    for begin, end in zip(CUTS, CUTS[1:] + (max_steps,)):

        @pl.when(taken > begin)
        def _():
            for step in range(begin, end):
                one_step(step)

    shape = (places, places * query_tokens)
    own = lax.broadcasted_iota(jnp.int32, shape, 1) // query_tokens
    own = (own == lax.broadcasted_iota(jnp.int32, shape, 0)).astype(jnp.float32)
    parts = lax.dot_general(
        own.astype(jnp.bfloat16),
        jnp.concatenate(pieces(tops[...]), axis=0),
        (((1,), (1,)), ((), ())),
        preferred_element_type=jnp.float32,
    )
    rows_of = 2 * max_steps
    sums = parts[:, :rows_of] + parts[:, rows_of : 2 * rows_of] + parts[:, 2 * rows_of :]
    by_step = in_step[:max_steps]
    spread = [
        exact_dot(sums[:, at * max_steps : (at + 1) * max_steps], by_step, ((1,), (0,)))
        for at in range(2)
    ]
    exact = jnp.sum(jnp.where(here, spread[0], 0.0), axis=0, keepdims=True)
    approx = jnp.sum(jnp.where(here, spread[1], 0.0), axis=0, keepdims=True)
    shape = (shards, 2 * pairs)
    pair = lax.broadcasted_iota(jnp.int32, shape, 1)
    from_shard = pair % pairs // cap == lax.broadcasted_iota(jnp.int32, shape, 0)
    scores = jnp.where(from_shard, jnp.concatenate([exact, approx], axis=1), 0.0)
    shape = (LANES, 2 * pairs)
    pair = lax.broadcasted_iota(jnp.int32, shape, 1)
    lane = pair // pairs * (LANES // 2) + pair % cap
    to_lane = (lax.broadcasted_iota(jnp.int32, shape, 0) == lane).astype(jnp.float32)
    back = exact_dot(scores, to_lane, ((1,), (1,)))
    for k, offset in enumerate(offsets):
        out[jnp.bitwise_xor(me, offset)] = back[k : k + 1, :]


def score(blocks, rows, offsets, query_tokens, cap, ways):
    passages, doubled, width = rows.shape
    shards = len(offsets)
    places = SIDES * PACK
    max_steps = -(-(shards * cap + (PACK - 1) * passages) // (8 * places)) * 8
    return pl.pallas_call(
        functools.partial(score_kernel, query_tokens, cap, ways, offsets),
        out_shape=pltpu.VMEM((shards, 1, LANES), jnp.float32),
        scratch_shapes=[
            pltpu.VMEM((places, LANES), jnp.int32),
            pltpu.SMEM((places, LANES), jnp.int32),
            pltpu.VMEM((2 * max_steps, places * query_tokens), jnp.float32),
            pltpu.SemaphoreType.DMA,
        ],
        compiler_params=pltpu.CompilerParams(vmem_limit_bytes=48 * 2**20),
        cost_estimate=pl.CostEstimate(
            flops=2 * max_steps * places * query_tokens * doubled * width,
            bytes_accessed=2 * (blocks.size + rows.size),
            transcendentals=0,
        ),
    )(blocks, rows)


def pick_kernel(plan, scores, exact_out, approx_out):
    q_local, top_k = exact_out.shape
    shards, padded, lanes = scores.shape
    slots = q_local * top_k
    target = plan[0:1, :]
    rank = plan[1:2, :]
    source = lax.broadcasted_iota(jnp.int32, (shards * padded, slots), 0)
    hot = (source == target * padded).astype(jnp.bfloat16)
    values = scores[...].reshape(shards * padded, lanes)
    spread = sum(
        lax.dot_general(
            part, hot, (((0,), (0,)), ((), ())), preferred_element_type=jnp.float32
        )
        for part in pieces(values)
    )
    lane = lax.broadcasted_iota(jnp.int32, (lanes, slots), 0)
    exact = jnp.sum(jnp.where(lane == rank, spread, 0.0), axis=0, keepdims=True)
    approx = jnp.sum(jnp.where(lane == rank + lanes // 2, spread, 0.0), axis=0, keepdims=True)
    for q in range(q_local):
        exact_out[q : q + 1, :] = exact[:, q * top_k : (q + 1) * top_k]
        approx_out[q : q + 1, :] = approx[:, q * top_k : (q + 1) * top_k]


def pick(plan, scores, shape):
    result = jax.ShapeDtypeStruct(shape, jnp.float32)
    operands = [pltpu.with_memory_space_constraint(x, pltpu.VMEM) for x in (plan, scores)]
    return pl.pallas_call(pick_kernel, out_shape=(result, result))(*operands)


def exchange(block, steps, shards):
    others = [
        lax.ppermute(block, "shard", [(i, i ^ step) for i in range(shards)]) for step in steps
    ]
    return [block] + others


def per_device(queries, centroids, codes, residual_codes, lengths, bucket_weights, candidates):
    shards = lax.axis_size("shard")
    passages = codes.shape[0]
    q_local, query_tokens, width = queries.shape
    tokens = q_local * query_tokens
    cap = max(2, 2 * candidates.size // shards)
    first_ways = 4 if shards % 4 == 0 else 2
    block, plan = make_plan(
        queries.reshape(tokens, width), candidates, shards, cap, passages, first_ways
    )
    block, codes = lax.optimization_barrier((block, codes))
    early = fetch(lengths, bucket_weights, codes, residual_codes, centroids, first_ways)
    offsets = [0]
    stride = shards
    while stride > 1:
        ways = 4 if stride % 4 == 0 else 2
        steps = [stride // ways * k for k in range(ways - 1, 0, -1)]
        blocks = exchange(block, steps, shards)
        if stride == shards:
            block = jnp.concatenate([x[:tokens] for x in blocks] + [sum(x[tokens:] for x in blocks)])
        else:
            block = jnp.concatenate(blocks)
        offsets = [k ^ at for k in [0] + steps for at in offsets]
        stride //= ways
        if stride > 1:
            block, lengths = lax.optimization_barrier((block, lengths))
    rows = decompress(
        lengths, bucket_weights, codes, residual_codes, centroids, first_ways, early
    )
    blocks = block.reshape(shards // first_ways, first_ways * tokens + META, width)
    scores = score(blocks, rows, offsets, query_tokens, cap, first_ways)
    back = lax.all_to_all(scores, "shard", split_axis=0, concat_axis=0, tiled=True)
    return pick(plan, back, candidates.shape)


def solution(mesh):
    placed = (
        P(("rep", "shard"), None, None),
        P("shard", None),
        P("shard", None),
        P("shard", None, None),
        P("shard"),
        P(),
        P(("rep", "shard"), None),
    )
    return jax.shard_map(
        per_device,
        mesh=mesh,
        in_specs=placed,
        out_specs=(P(("rep", "shard"), None), P(("rep", "shard"), None)),
        check_vma=False,
    )
```

```python
import functools

import jax
import jax.numpy as jnp
from jax import lax
from jax.experimental import pallas as pl
from jax.experimental.pallas import tpu as pltpu
from jax.sharding import PartitionSpec as P

GROUP = 256
DEAD = 1 << 16
STEP = 4
META = 16
LANES = 128
PACK = 4
SIDES = 2
CUTS = (0, 24, 40)


def start_copies(sources, targets, sems):
    copies = [
        pltpu.make_async_copy(source, target, sems.at[i])
        for i, (source, target) in enumerate(zip(sources, targets))
    ]
    for copy in copies:
        copy.start()
    return copies


def prepare(copies, lengths_row, codes, centroids, weights, hot, high, table, levels):
    passages, slots = codes.shape
    count, width = centroids.shape
    copies[0].wait()
    copies[1].wait()
    columns = jnp.swapaxes(codes[...].astype(jnp.float32), 0, 1).astype(jnp.int32)
    live = lax.broadcasted_iota(jnp.int32, columns.shape, 0) < lengths_row[...]
    columns = jnp.where(live, columns, columns[0:1, :])
    low = columns % GROUP
    top = jnp.where(live, columns // GROUP, columns // GROUP + DEAD)
    lane = lax.broadcasted_iota(jnp.int32, (slots, GROUP), 1)
    for p in range(passages):
        at = slice(p * slots, (p + 1) * slots)
        hot[at, :] = (lane == low[:, p : p + 1]).astype(jnp.bfloat16)
        high[at, :] = jnp.broadcast_to(top[:, p : p + 1], (slots, width))
    copies[2].wait()
    for g in range(count // GROUP):
        table[:, g * width : (g + 1) * width] = centroids[g * GROUP : (g + 1) * GROUP, :]
    for copy in copies[3:]:
        copy.wait()
    for k in range(weights.shape[0]):
        levels[k : k + 1, :] = jnp.full((1, width), weights[k])


def build_rows(first, residuals, hot, high, table, levels, rows):
    _, slots, width = residuals.shape
    groups = table.shape[1] // width
    level = [jnp.broadcast_to(levels[k : k + 1, :], (slots, width)) for k in range(4)]
    spread = jnp.dot(
        hot[first * slots : (first + STEP) * slots, :],
        table[...],
        preferred_element_type=jnp.float32,
    )
    for p in range(first, first + STEP):
        at = p - first
        part = spread[at * slots : (at + 1) * slots]
        choice = [part[:, g * width : (g + 1) * width] for g in range(groups)]
        group = high[p * slots : (p + 1) * slots, :]
        bit = 1
        while len(choice) > 1:
            odd = (group & bit) != 0
            choice = [jnp.where(odd, choice[k + 1], choice[k]) for k in range(0, len(choice), 2)]
            bit *= 2
        cent = choice[0]
        code = residuals[p]
        code = jnp.where(group < DEAD, code, code[0:1, :])
        odd = (code & 1) == 1
        low = jnp.where(odd, level[1], level[0])
        top = jnp.where(odd, level[3], level[2])
        values = cent + jnp.where(code >= 2, top, low)
        norm = lax.rsqrt(jnp.sum(values * values, axis=-1, keepdims=True) + 1e-06)
        rows[p, :slots, :] = (values * norm).astype(jnp.bfloat16)
        rows[p, slots:, :] = cent.astype(jnp.bfloat16)


def fetches_late(ways):
    shards = lax.axis_size("shard")
    odd_member = lax.axis_index("shard") // (shards // ways) % 2 == 1
    return jnp.logical_and(odd_member, lax.axis_index("rep") % 2 == 1)


def fetch_kernel(ways, *refs):
    sources = refs[:5]
    residuals, hot, high, table, levels = refs[5:10]
    lengths_row, codes, centroids, weights, sems = refs[10:]

    @pl.when(jnp.logical_not(fetches_late(ways)))
    def _():
        targets = (lengths_row, codes, centroids, weights, residuals)
        copies = start_copies(sources, targets, sems)
        prepare(copies, lengths_row, codes, centroids, weights, hot, high, table, levels)


def index_scratch(lengths, bucket_weights, codes, centroids, count):
    return [
        pltpu.VMEM((1, lengths.shape[0]), lengths.dtype),
        pltpu.VMEM(codes.shape, codes.dtype),
        pltpu.VMEM(centroids.shape, centroids.dtype),
        pltpu.SMEM(bucket_weights.shape, bucket_weights.dtype),
        pltpu.SemaphoreType.DMA((count,)),
    ]


def index_arrays(codes, centroids, width):
    tokens = codes.size
    return [
        pltpu.VMEM(codes.shape + (width,), jnp.int32),
        pltpu.VMEM((tokens, GROUP), jnp.bfloat16),
        pltpu.VMEM((tokens, width), jnp.int32),
        pltpu.VMEM((GROUP, centroids.size // GROUP), jnp.bfloat16),
        pltpu.VMEM((8, width), jnp.float32),
    ]


def fetch(lengths, bucket_weights, codes, residual_codes, centroids, ways):
    passages = codes.shape[0]
    width = centroids.shape[1]
    operands = (
        lengths.reshape(1, passages), codes, centroids, bucket_weights, residual_codes
    )
    return pl.pallas_call(
        functools.partial(fetch_kernel, ways),
        in_specs=[pl.BlockSpec(memory_space=pltpu.HBM)] * len(operands),
        out_specs=[pl.BlockSpec(memory_space=pltpu.VMEM)] * 5,
        out_shape=index_arrays(codes, centroids, width),
        scratch_shapes=index_scratch(lengths, bucket_weights, codes, centroids, len(operands)),
        compiler_params=pltpu.CompilerParams(vmem_limit_bytes=32 * 2**20),
        cost_estimate=pl.CostEstimate(
            flops=0, bytes_accessed=2 * residual_codes.nbytes, transcendentals=0
        ),
    )(*[pltpu.with_memory_space_constraint(x, pltpu.HBM) for x in operands])


def decompress_kernel(ways, *refs):
    sources = refs[:5]
    early = refs[5:10]
    rows = refs[10]
    lengths_row, codes, centroids, weights, sems = refs[11:16]
    own = refs[16:]
    passages = codes.shape[0]
    late = fetches_late(ways)

    @pl.when(jnp.logical_not(late))
    def _():
        for first in range(0, passages, STEP):
            build_rows(first, *early, rows)

    @pl.when(late)
    def _():
        targets = (lengths_row, codes, centroids, weights, own[0])
        copies = start_copies(sources, targets, sems)
        prepare(copies, lengths_row, codes, centroids, weights, *own[1:])
        for first in range(0, passages, STEP):
            build_rows(first, *own, rows)


def decompress(lengths, bucket_weights, codes, residual_codes, centroids, ways, early):
    passages, slots = codes.shape
    width = centroids.shape[1]
    operands = (
        lengths.reshape(1, passages), codes, centroids, bucket_weights, residual_codes
    )
    return pl.pallas_call(
        functools.partial(decompress_kernel, ways),
        in_specs=[pl.BlockSpec(memory_space=pltpu.HBM)] * len(operands)
        + [pl.BlockSpec(memory_space=pltpu.VMEM)] * len(early),
        out_specs=pl.BlockSpec(memory_space=pltpu.VMEM),
        out_shape=pltpu.VMEM((passages, 2 * slots, width), jnp.bfloat16),
        scratch_shapes=index_scratch(lengths, bucket_weights, codes, centroids, len(operands))
        + index_arrays(codes, centroids, width),
        compiler_params=pltpu.CompilerParams(vmem_limit_bytes=40 * 2**20),
        cost_estimate=pl.CostEstimate(
            flops=2 * codes.size * centroids.size,
            bytes_accessed=4 * codes.size * width,
            transcendentals=0,
        ),
    )(
        *[pltpu.with_memory_space_constraint(x, pltpu.HBM) for x in operands],
        *[pltpu.with_memory_space_constraint(x, pltpu.VMEM) for x in early],
    )


def plan_kernel(shards, cap, passages, ways, queries_hbm, candidates_hbm, block, plan, candidates, query_sem, cand_sem):
    q_local, top_k = candidates.shape
    tokens = queries_hbm.shape[0]
    send_queries = pltpu.make_async_copy(queries_hbm, block.at[pl.ds(0, tokens)], query_sem)
    get_candidates = pltpu.make_async_copy(candidates_hbm, candidates, cand_sem)
    get_candidates.start()
    send_queries.start()
    get_candidates.wait()
    slots = q_local * top_k
    per_row = shards // META
    cand = jnp.concatenate([candidates[q : q + 1, :] for q in range(q_local)], axis=1)
    target = cand // passages
    value = lax.broadcasted_iota(jnp.int32, (1, slots), 1) // top_k * passages + cand % passages + 1
    square = (slots, slots)
    wide = jnp.broadcast_to(target.astype(jnp.float32), square)
    earlier = lax.broadcasted_iota(jnp.int32, square, 0) < lax.broadcasted_iota(
        jnp.int32, square, 1
    )
    same = (jnp.swapaxes(wide, 0, 1) == wide) & earlier
    rank = jnp.sum(same.astype(jnp.int32), axis=0, keepdims=True)
    row = lax.broadcasted_iota(jnp.int32, (META, slots), 0)
    left = jnp.where(row == target // per_row, value.astype(jnp.float32), 0.0)
    digit = lax.axis_index("shard") // (shards // ways)
    lane = lax.broadcasted_iota(jnp.int32, (LANES, slots), 0) - digit * (per_row * cap)
    right = (lane == target % per_row * cap + rank).astype(jnp.float32)
    lists = lax.dot_general(
        left.astype(jnp.bfloat16),
        right.astype(jnp.bfloat16),
        (((1,), (1,)), ((), ())),
        preferred_element_type=jnp.float32,
    )
    block[tokens:, :] = lists.astype(jnp.bfloat16)
    plan[0:1, :] = target
    plan[1:2, :] = rank
    send_queries.wait()


def make_plan(queries, candidates, shards, cap, passages, ways):
    tokens, width = queries.shape
    operands = (queries, candidates)
    return pl.pallas_call(
        functools.partial(plan_kernel, shards, cap, passages, ways),
        in_specs=[pl.BlockSpec(memory_space=pltpu.HBM)] * 2,
        out_specs=[pl.BlockSpec(memory_space=pltpu.VMEM)] * 2,
        out_shape=(
            pltpu.VMEM((tokens + META, width), jnp.bfloat16),
            pltpu.VMEM((8, candidates.size), jnp.int32),
        ),
        scratch_shapes=[
            pltpu.VMEM(candidates.shape, candidates.dtype),
            pltpu.SemaphoreType.DMA,
            pltpu.SemaphoreType.DMA,
        ],
    )(*[pltpu.with_memory_space_constraint(x, pltpu.HBM) for x in operands])


def pieces(values):
    high = values.astype(jnp.bfloat16)
    rest = values - high.astype(jnp.float32)
    middle = rest.astype(jnp.bfloat16)
    low = (rest - middle.astype(jnp.float32)).astype(jnp.bfloat16)
    return [high, middle, low]


def exact_dot(values, mask, dims):
    rows = values.shape[0]
    parts = lax.dot_general(
        jnp.concatenate(pieces(values), axis=0),
        mask.astype(jnp.bfloat16),
        (dims, ((), ())),
        preferred_element_type=jnp.float32,
    )
    return parts[:rows] + parts[rows : 2 * rows] + parts[2 * rows :]


def score_kernel(query_tokens, cap, ways, offsets, blocks, rows, out, listed, steps, tops, sem):
    passages, doubled, width = rows.shape
    slots = doubled // 2
    outer, block_rows, _ = blocks.shape
    shards = len(offsets)
    shard_rows = (block_rows - META) // ways
    per_row = shards // META
    me = lax.axis_index("shard")
    pairs = shards * cap
    max_steps = tops.shape[0] // 2
    bits = (passages - 1).bit_length()
    span = 1 << bits

    lists = blocks[:, block_rows - META :, :].reshape(outer * META, LANES)
    shape = (pairs, outer * META)
    pair = lax.broadcasted_iota(jnp.int32, shape, 0)
    wanted = pair // (cap * ways) * META + me // per_row
    pick = (lax.broadcasted_iota(jnp.int32, shape, 1) == wanted).astype(jnp.bfloat16)
    found = jnp.dot(pick, lists, preferred_element_type=jnp.float32)
    shape = (pairs, LANES)
    pair = lax.broadcasted_iota(jnp.int32, shape, 0)
    digit = jnp.bitwise_xor(me // (shards // ways), (ways - pair // cap % ways) % ways)
    lane = (digit * per_row + me % per_row) * cap + pair % cap
    own = lax.broadcasted_iota(jnp.int32, shape, 1) == lane
    column = jnp.sum(jnp.where(own, found, 0.0), axis=1, keepdims=True)
    wide = jnp.broadcast_to(column, shape)
    code_row = jnp.swapaxes(wide, 0, 1)[0:1, :].astype(jnp.int32)
    code_col = wide.astype(jnp.int32)

    def passage_of(code):
        return jnp.where(code > 0, (code - 1) % passages, passages)

    valid = code_row > 0
    p_row = passage_of(code_row)
    p_col = passage_of(code_col)[:, 0:1]
    square = (pairs, pairs)
    earlier = lax.broadcasted_iota(jnp.int32, square, 0) < lax.broadcasted_iota(
        jnp.int32, square, 1
    )
    rank = jnp.sum(((p_col == p_row) & earlier).astype(jnp.int32), axis=0, keepdims=True)
    shape = (passages, pairs)
    p_iota = lax.broadcasted_iota(jnp.int32, shape, 0)
    count = jnp.sum((p_iota == p_row).astype(jnp.int32), axis=1, keepdims=True)
    need = (count + PACK - 1) // PACK
    start = jnp.sum(jnp.where(p_iota < p_row, need, 0), axis=0, keepdims=True)
    half = start + rank // PACK
    step_row = jnp.where(valid, half // SIDES, max_steps)
    place_row = half % SIDES * PACK + rank % PACK
    pair_row = lax.broadcasted_iota(jnp.int32, (1, pairs), 1)
    query_row = (
        pair_row // (cap * ways) * (block_rows // 16)
        + pair_row // cap % ways * (shard_rows // 16)
        + (code_row - 1) // passages * (query_tokens // 16)
    )
    entry = jnp.where(valid, query_row * span + p_row, 0).astype(jnp.float32)
    in_step = lax.broadcasted_iota(jnp.int32, (LANES, pairs), 0) == step_row
    in_step = in_step.astype(jnp.float32)
    places = SIDES * PACK
    here = lax.broadcasted_iota(jnp.int32, (places, pairs), 0) == place_row
    entries = exact_dot(jnp.where(here, entry, 0.0), in_step, ((1,), (1,)))
    total = jnp.sum(need, axis=0, keepdims=True)
    lane = lax.broadcasted_iota(jnp.int32, (places, LANES), 1)
    total = (total + SIDES - 1) // SIDES
    listed[...] = jnp.where(lane == LANES - 1, total, entries.astype(jnp.int32))
    copy = pltpu.make_async_copy(listed, steps, sem)
    copy.start()
    tops[...] = jnp.zeros_like(tops)
    copy.wait()

    flat = blocks.reshape(outer * block_rows, width)

    blank = jnp.zeros((PACK * query_tokens, width), jnp.bfloat16)

    def one_step(step):
        sides = []
        packed = []
        for side in range(SIDES):
            first = side * PACK
            sides.append(rows[steps[first, step] & (span - 1)])
            queries = jnp.concatenate(
                [
                    flat[pl.ds(pl.multiple_of((steps[k, step] >> bits) * 16, 16), query_tokens), :]
                    for k in range(first, first + PACK)
                ],
                axis=0,
            )
            packed.append(
                jnp.concatenate([queries if at == side else blank for at in range(SIDES)], axis=1)
            )
        dots = lax.dot_general(
            jnp.concatenate(sides, axis=1),
            jnp.concatenate(packed, axis=0),
            (((1,), (1,)), ((), ())),
            preferred_element_type=jnp.float32,
        )
        best = jnp.max(dots.reshape(2, slots, places * query_tokens), axis=1)
        tops[step : step + 1, :] = best[0:1]
        tops[max_steps + step : max_steps + step + 1, :] = best[1:2]

    taken = steps[0, LANES - 1]
    for begin, end in zip(CUTS, CUTS[1:] + (max_steps,)):

        @pl.when(taken > begin)
        def _():
            for step in range(begin, end):
                one_step(step)

    shape = (places, places * query_tokens)
    own = lax.broadcasted_iota(jnp.int32, shape, 1) // query_tokens
    own = (own == lax.broadcasted_iota(jnp.int32, shape, 0)).astype(jnp.float32)
    parts = lax.dot_general(
        own.astype(jnp.bfloat16),
        jnp.concatenate(pieces(tops[...]), axis=0),
        (((1,), (1,)), ((), ())),
        preferred_element_type=jnp.float32,
    )
    rows_of = 2 * max_steps
    sums = parts[:, :rows_of] + parts[:, rows_of : 2 * rows_of] + parts[:, 2 * rows_of :]
    by_step = in_step[:max_steps]
    spread = [
        exact_dot(sums[:, at * max_steps : (at + 1) * max_steps], by_step, ((1,), (0,)))
        for at in range(2)
    ]
    exact = jnp.sum(jnp.where(here, spread[0], 0.0), axis=0, keepdims=True)
    approx = jnp.sum(jnp.where(here, spread[1], 0.0), axis=0, keepdims=True)
    shape = (shards, 2 * pairs)
    pair = lax.broadcasted_iota(jnp.int32, shape, 1)
    from_shard = pair % pairs // cap == lax.broadcasted_iota(jnp.int32, shape, 0)
    scores = jnp.where(from_shard, jnp.concatenate([exact, approx], axis=1), 0.0)
    shape = (LANES, 2 * pairs)
    pair = lax.broadcasted_iota(jnp.int32, shape, 1)
    lane = pair // pairs * (LANES // 2) + pair % cap
    to_lane = (lax.broadcasted_iota(jnp.int32, shape, 0) == lane).astype(jnp.float32)
    back = exact_dot(scores, to_lane, ((1,), (1,)))
    for k, offset in enumerate(offsets):
        out[jnp.bitwise_xor(me, offset)] = back[k : k + 1, :]


def score(blocks, rows, offsets, query_tokens, cap, ways):
    passages, doubled, width = rows.shape
    shards = len(offsets)
    places = SIDES * PACK
    max_steps = -(-(shards * cap + (PACK - 1) * passages) // (8 * places)) * 8
    return pl.pallas_call(
        functools.partial(score_kernel, query_tokens, cap, ways, offsets),
        out_shape=pltpu.VMEM((shards, 1, LANES), jnp.float32),
        scratch_shapes=[
            pltpu.VMEM((places, LANES), jnp.int32),
            pltpu.SMEM((places, LANES), jnp.int32),
            pltpu.VMEM((2 * max_steps, places * query_tokens), jnp.float32),
            pltpu.SemaphoreType.DMA,
        ],
        compiler_params=pltpu.CompilerParams(vmem_limit_bytes=48 * 2**20),
        cost_estimate=pl.CostEstimate(
            flops=2 * max_steps * places * query_tokens * doubled * width,
            bytes_accessed=2 * (blocks.size + rows.size),
            transcendentals=0,
        ),
    )(blocks, rows)


def pick_kernel(plan, scores, exact_out, approx_out):
    q_local, top_k = exact_out.shape
    shards, padded, lanes = scores.shape
    slots = q_local * top_k
    target = plan[0:1, :]
    rank = plan[1:2, :]
    source = lax.broadcasted_iota(jnp.int32, (shards * padded, slots), 0)
    hot = (source == target * padded).astype(jnp.bfloat16)
    values = scores[...].reshape(shards * padded, lanes)
    spread = sum(
        lax.dot_general(
            part, hot, (((0,), (0,)), ((), ())), preferred_element_type=jnp.float32
        )
        for part in pieces(values)
    )
    lane = lax.broadcasted_iota(jnp.int32, (lanes, slots), 0)
    exact = jnp.sum(jnp.where(lane == rank, spread, 0.0), axis=0, keepdims=True)
    approx = jnp.sum(jnp.where(lane == rank + lanes // 2, spread, 0.0), axis=0, keepdims=True)
    for q in range(q_local):
        exact_out[q : q + 1, :] = exact[:, q * top_k : (q + 1) * top_k]
        approx_out[q : q + 1, :] = approx[:, q * top_k : (q + 1) * top_k]


def pick(plan, scores, shape):
    result = jax.ShapeDtypeStruct(shape, jnp.float32)
    operands = [pltpu.with_memory_space_constraint(x, pltpu.VMEM) for x in (plan, scores)]
    return pl.pallas_call(pick_kernel, out_shape=(result, result))(*operands)


def exchange(block, steps, shards):
    others = [
        lax.ppermute(block, "shard", [(i, i ^ step) for i in range(shards)]) for step in steps
    ]
    return [block] + others


def per_device(queries, centroids, codes, residual_codes, lengths, bucket_weights, candidates):
    shards = lax.axis_size("shard")
    passages = codes.shape[0]
    q_local, query_tokens, width = queries.shape
    tokens = q_local * query_tokens
    cap = max(2, 2 * candidates.size // shards)
    first_ways = 4 if shards % 4 == 0 else 2
    block, plan = make_plan(
        queries.reshape(tokens, width), candidates, shards, cap, passages, first_ways
    )
    block, codes = lax.optimization_barrier((block, codes))
    early = fetch(lengths, bucket_weights, codes, residual_codes, centroids, first_ways)
    offsets = [0]
    stride = shards
    while stride > 1:
        ways = 4 if stride % 4 == 0 else 2
        steps = [stride // ways * k for k in range(ways - 1, 0, -1)]
        blocks = exchange(block, steps, shards)
        if stride == shards:
            block = jnp.concatenate([x[:tokens] for x in blocks] + [sum(x[tokens:] for x in blocks)])
        else:
            block = jnp.concatenate(blocks)
        offsets = [k ^ at for k in [0] + steps for at in offsets]
        stride //= ways
        if stride > 1:
            block, lengths = lax.optimization_barrier((block, lengths))
    rows = decompress(
        lengths, bucket_weights, codes, residual_codes, centroids, first_ways, early
    )
    blocks = block.reshape(shards // first_ways, first_ways * tokens + META, width)
    scores = score(blocks, rows, offsets, query_tokens, cap, first_ways)
    back = lax.all_to_all(scores, "shard", split_axis=0, concat_axis=0, tiled=True)
    return pick(plan, back, candidates.shape)


def solution(mesh):
    placed = (
        P(("rep", "shard"), None, None),
        P("shard", None),
        P("shard", None),
        P("shard", None, None),
        P("shard"),
        P(),
        P(("rep", "shard"), None),
    )
    return jax.shard_map(
        per_device,
        mesh=mesh,
        in_specs=placed,
        out_specs=(P(("rep", "shard"), None), P(("rep", "shard"), None)),
        check_vma=False,
    )
```

```python
import functools

import jax
import jax.numpy as jnp
from jax import lax
from jax.experimental import pallas as pl
from jax.experimental.pallas import tpu as pltpu
from jax.sharding import PartitionSpec as P

GROUP = 256
DEAD = 1 << 16
STEP = 4
META = 16
LANES = 128
PACK = 4
SIDES = 2
CUTS = (0, 24, 40)


def start_copies(sources, targets, sems):
    copies = [
        pltpu.make_async_copy(source, target, sems.at[i])
        for i, (source, target) in enumerate(zip(sources, targets))
    ]
    for copy in copies:
        copy.start()
    return copies


def prepare(copies, lengths_row, codes, centroids, weights, hot, high, table, levels, lows):
    passages, slots = codes.shape
    count, width = centroids.shape
    copies[0].wait()
    copies[1].wait()
    columns = jnp.swapaxes(codes[...].astype(jnp.float32), 0, 1).astype(jnp.int32)
    live = lax.broadcasted_iota(jnp.int32, columns.shape, 0) < lengths_row[...]
    columns = jnp.where(live, columns, columns[0:1, :])
    low = columns % GROUP
    top = jnp.where(live, columns // GROUP, columns // GROUP + DEAD)
    lows[...] = low
    lane = lax.broadcasted_iota(jnp.int32, (slots, GROUP), 1)
    for p in range(passages):
        at = slice(p * slots, (p + 1) * slots)
        if p < passages // 2:
            hot[at, :] = (lane == low[:, p : p + 1]).astype(jnp.bfloat16)
        high[at, :] = jnp.broadcast_to(top[:, p : p + 1], (slots, width))
    copies[2].wait()
    for g in range(count // GROUP):
        table[:, g * width : (g + 1) * width] = centroids[g * GROUP : (g + 1) * GROUP, :]
    for copy in copies[3:]:
        copy.wait()
    for k in range(weights.shape[0]):
        levels[k : k + 1, :] = jnp.full((1, width), weights[k])


def build_rows(first, residuals, hot, high, table, levels, lows, rows):
    _, slots, width = residuals.shape
    groups = table.shape[1] // width
    level = [jnp.broadcast_to(levels[k : k + 1, :], (slots, width)) for k in range(4)]
    if first < residuals.shape[0] // 2:
        chosen = hot[first * slots : (first + STEP) * slots, :]
    else:
        lane = lax.broadcasted_iota(jnp.int32, (slots, GROUP), 1)
        chosen = jnp.concatenate(
            [(lane == lows[:, p : p + 1]).astype(jnp.bfloat16) for p in range(first, first + STEP)]
        )
    spread = jnp.dot(
        chosen,
        table[...],
        preferred_element_type=jnp.float32,
    )
    for p in range(first, first + STEP):
        at = p - first
        part = spread[at * slots : (at + 1) * slots]
        choice = [part[:, g * width : (g + 1) * width] for g in range(groups)]
        group = high[p * slots : (p + 1) * slots, :]
        bit = 1
        while len(choice) > 1:
            odd = (group & bit) != 0
            choice = [jnp.where(odd, choice[k + 1], choice[k]) for k in range(0, len(choice), 2)]
            bit *= 2
        cent = choice[0]
        code = residuals[p]
        code = jnp.where(group < DEAD, code, code[0:1, :])
        odd = (code & 1) == 1
        low = jnp.where(odd, level[1], level[0])
        top = jnp.where(odd, level[3], level[2])
        values = cent + jnp.where(code >= 2, top, low)
        norm = lax.rsqrt(jnp.sum(values * values, axis=-1, keepdims=True) + 1e-06)
        rows[p, :slots, :] = (values * norm).astype(jnp.bfloat16)
        rows[p, slots:, :] = cent.astype(jnp.bfloat16)


def fetches_late(ways):
    shards = lax.axis_size("shard")
    odd_member = lax.axis_index("shard") // (shards // ways) % 2 == 1
    return jnp.logical_and(odd_member, lax.axis_index("rep") % 2 == 1)


def fetch_kernel(ways, *refs):
    sources = refs[:5]
    residuals, hot, high, table, levels, lows = refs[5:11]
    lengths_row, codes, centroids, weights, sems = refs[11:]

    @pl.when(jnp.logical_not(fetches_late(ways)))
    def _():
        targets = (lengths_row, codes, centroids, weights, residuals)
        copies = start_copies(sources, targets, sems)
        prepare(copies, lengths_row, codes, centroids, weights, hot, high, table, levels, lows)


def index_scratch(lengths, bucket_weights, codes, centroids, count):
    return [
        pltpu.VMEM((1, lengths.shape[0]), lengths.dtype),
        pltpu.VMEM(codes.shape, codes.dtype),
        pltpu.VMEM(centroids.shape, centroids.dtype),
        pltpu.SMEM(bucket_weights.shape, bucket_weights.dtype),
        pltpu.SemaphoreType.DMA((count,)),
    ]


def index_arrays(codes, centroids, width):
    tokens = codes.size
    return [
        pltpu.VMEM(codes.shape + (width,), jnp.int32),
        pltpu.VMEM((tokens, GROUP), jnp.bfloat16),
        pltpu.VMEM((tokens, width), jnp.int32),
        pltpu.VMEM((GROUP, centroids.size // GROUP), jnp.bfloat16),
        pltpu.VMEM((8, width), jnp.float32),
        pltpu.VMEM(codes.shape[::-1], jnp.int32),
    ]


def fetch(lengths, bucket_weights, codes, residual_codes, centroids, ways):
    passages = codes.shape[0]
    width = centroids.shape[1]
    operands = (
        lengths.reshape(1, passages), codes, centroids, bucket_weights, residual_codes
    )
    return pl.pallas_call(
        functools.partial(fetch_kernel, ways),
        in_specs=[pl.BlockSpec(memory_space=pltpu.HBM)] * len(operands),
        out_specs=[pl.BlockSpec(memory_space=pltpu.VMEM)] * 6,
        out_shape=index_arrays(codes, centroids, width),
        scratch_shapes=index_scratch(lengths, bucket_weights, codes, centroids, len(operands)),
        compiler_params=pltpu.CompilerParams(vmem_limit_bytes=32 * 2**20),
        cost_estimate=pl.CostEstimate(
            flops=0, bytes_accessed=2 * residual_codes.nbytes, transcendentals=0
        ),
    )(*[pltpu.with_memory_space_constraint(x, pltpu.HBM) for x in operands])


def decompress_kernel(ways, *refs):
    sources = refs[:5]
    early = refs[5:11]
    rows = refs[11]
    lengths_row, codes, centroids, weights, sems = refs[12:17]
    own = refs[17:]
    passages = codes.shape[0]
    late = fetches_late(ways)

    @pl.when(jnp.logical_not(late))
    def _():
        for first in range(0, passages, STEP):
            build_rows(first, *early, rows)

    @pl.when(late)
    def _():
        targets = (lengths_row, codes, centroids, weights, own[0])
        copies = start_copies(sources, targets, sems)
        prepare(copies, lengths_row, codes, centroids, weights, *own[1:])
        for first in range(0, passages, STEP):
            build_rows(first, *own, rows)


def decompress(lengths, bucket_weights, codes, residual_codes, centroids, ways, early):
    passages, slots = codes.shape
    width = centroids.shape[1]
    operands = (
        lengths.reshape(1, passages), codes, centroids, bucket_weights, residual_codes
    )
    return pl.pallas_call(
        functools.partial(decompress_kernel, ways),
        in_specs=[pl.BlockSpec(memory_space=pltpu.HBM)] * len(operands)
        + [pl.BlockSpec(memory_space=pltpu.VMEM)] * len(early),
        out_specs=pl.BlockSpec(memory_space=pltpu.VMEM),
        out_shape=pltpu.VMEM((passages, 2 * slots, width), jnp.bfloat16),
        scratch_shapes=index_scratch(lengths, bucket_weights, codes, centroids, len(operands))
        + index_arrays(codes, centroids, width),
        compiler_params=pltpu.CompilerParams(vmem_limit_bytes=40 * 2**20),
        cost_estimate=pl.CostEstimate(
            flops=2 * codes.size * centroids.size,
            bytes_accessed=4 * codes.size * width,
            transcendentals=0,
        ),
    )(
        *[pltpu.with_memory_space_constraint(x, pltpu.HBM) for x in operands],
        *[pltpu.with_memory_space_constraint(x, pltpu.VMEM) for x in early],
    )


def plan_kernel(shards, cap, passages, ways, queries_hbm, candidates_hbm, block, plan, candidates, query_sem, cand_sem):
    q_local, top_k = candidates.shape
    tokens = queries_hbm.shape[0]
    send_queries = pltpu.make_async_copy(queries_hbm, block.at[pl.ds(0, tokens)], query_sem)
    get_candidates = pltpu.make_async_copy(candidates_hbm, candidates, cand_sem)
    get_candidates.start()
    send_queries.start()
    get_candidates.wait()
    slots = q_local * top_k
    per_row = shards // META
    cand = jnp.concatenate([candidates[q : q + 1, :] for q in range(q_local)], axis=1)
    target = cand // passages
    value = lax.broadcasted_iota(jnp.int32, (1, slots), 1) // top_k * passages + cand % passages + 1
    square = (slots, slots)
    wide = jnp.broadcast_to(target.astype(jnp.float32), square)
    earlier = lax.broadcasted_iota(jnp.int32, square, 0) < lax.broadcasted_iota(
        jnp.int32, square, 1
    )
    same = (jnp.swapaxes(wide, 0, 1) == wide) & earlier
    rank = jnp.sum(same.astype(jnp.int32), axis=0, keepdims=True)
    row = lax.broadcasted_iota(jnp.int32, (META, slots), 0)
    left = jnp.where(row == target // per_row, value.astype(jnp.float32), 0.0)
    digit = lax.axis_index("shard") // (shards // ways)
    lane = lax.broadcasted_iota(jnp.int32, (LANES, slots), 0) - digit * (per_row * cap)
    right = (lane == target % per_row * cap + rank).astype(jnp.float32)
    lists = lax.dot_general(
        left.astype(jnp.bfloat16),
        right.astype(jnp.bfloat16),
        (((1,), (1,)), ((), ())),
        preferred_element_type=jnp.float32,
    )
    block[tokens:, :] = lists.astype(jnp.bfloat16)
    plan[0:1, :] = target
    plan[1:2, :] = rank
    send_queries.wait()


def make_plan(queries, candidates, shards, cap, passages, ways):
    tokens, width = queries.shape
    operands = (queries, candidates)
    return pl.pallas_call(
        functools.partial(plan_kernel, shards, cap, passages, ways),
        in_specs=[pl.BlockSpec(memory_space=pltpu.HBM)] * 2,
        out_specs=[pl.BlockSpec(memory_space=pltpu.VMEM)] * 2,
        out_shape=(
            pltpu.VMEM((tokens + META, width), jnp.bfloat16),
            pltpu.VMEM((8, candidates.size), jnp.int32),
        ),
        scratch_shapes=[
            pltpu.VMEM(candidates.shape, candidates.dtype),
            pltpu.SemaphoreType.DMA,
            pltpu.SemaphoreType.DMA,
        ],
    )(*[pltpu.with_memory_space_constraint(x, pltpu.HBM) for x in operands])


def pieces(values):
    high = values.astype(jnp.bfloat16)
    rest = values - high.astype(jnp.float32)
    middle = rest.astype(jnp.bfloat16)
    low = (rest - middle.astype(jnp.float32)).astype(jnp.bfloat16)
    return [high, middle, low]


def exact_dot(values, mask, dims):
    rows = values.shape[0]
    parts = lax.dot_general(
        jnp.concatenate(pieces(values), axis=0),
        mask.astype(jnp.bfloat16),
        (dims, ((), ())),
        preferred_element_type=jnp.float32,
    )
    return parts[:rows] + parts[rows : 2 * rows] + parts[2 * rows :]


def score_kernel(query_tokens, cap, ways, offsets, blocks, rows, out, listed, steps, tops, sem):
    passages, doubled, width = rows.shape
    slots = doubled // 2
    outer, block_rows, _ = blocks.shape
    shards = len(offsets)
    shard_rows = (block_rows - META) // ways
    per_row = shards // META
    me = lax.axis_index("shard")
    pairs = shards * cap
    max_steps = tops.shape[0] // 2
    bits = (passages - 1).bit_length()
    span = 1 << bits

    lists = blocks[:, block_rows - META :, :].reshape(outer * META, LANES)
    shape = (pairs, outer * META)
    pair = lax.broadcasted_iota(jnp.int32, shape, 0)
    wanted = pair // (cap * ways) * META + me // per_row
    pick = (lax.broadcasted_iota(jnp.int32, shape, 1) == wanted).astype(jnp.bfloat16)
    found = jnp.dot(pick, lists, preferred_element_type=jnp.float32)
    shape = (pairs, LANES)
    pair = lax.broadcasted_iota(jnp.int32, shape, 0)
    digit = jnp.bitwise_xor(me // (shards // ways), (ways - pair // cap % ways) % ways)
    lane = (digit * per_row + me % per_row) * cap + pair % cap
    own = lax.broadcasted_iota(jnp.int32, shape, 1) == lane
    column = jnp.sum(jnp.where(own, found, 0.0), axis=1, keepdims=True)
    wide = jnp.broadcast_to(column, shape)
    code_row = jnp.swapaxes(wide, 0, 1)[0:1, :].astype(jnp.int32)
    code_col = wide.astype(jnp.int32)

    def passage_of(code):
        return jnp.where(code > 0, (code - 1) % passages, passages)

    valid = code_row > 0
    p_row = passage_of(code_row)
    p_col = passage_of(code_col)[:, 0:1]
    square = (pairs, pairs)
    earlier = lax.broadcasted_iota(jnp.int32, square, 0) < lax.broadcasted_iota(
        jnp.int32, square, 1
    )
    rank = jnp.sum(((p_col == p_row) & earlier).astype(jnp.int32), axis=0, keepdims=True)
    shape = (passages, pairs)
    p_iota = lax.broadcasted_iota(jnp.int32, shape, 0)
    count = jnp.sum((p_iota == p_row).astype(jnp.int32), axis=1, keepdims=True)
    need = (count + PACK - 1) // PACK
    start = jnp.sum(jnp.where(p_iota < p_row, need, 0), axis=0, keepdims=True)
    half = start + rank // PACK
    step_row = jnp.where(valid, half // SIDES, max_steps)
    place_row = half % SIDES * PACK + rank % PACK
    pair_row = lax.broadcasted_iota(jnp.int32, (1, pairs), 1)
    query_row = (
        pair_row // (cap * ways) * (block_rows // 16)
        + pair_row // cap % ways * (shard_rows // 16)
        + (code_row - 1) // passages * (query_tokens // 16)
    )
    entry = jnp.where(valid, query_row * span + p_row, 0).astype(jnp.float32)
    in_step = lax.broadcasted_iota(jnp.int32, (LANES, pairs), 0) == step_row
    in_step = in_step.astype(jnp.float32)
    places = SIDES * PACK
    here = lax.broadcasted_iota(jnp.int32, (places, pairs), 0) == place_row
    entries = exact_dot(jnp.where(here, entry, 0.0), in_step, ((1,), (1,)))
    total = jnp.sum(need, axis=0, keepdims=True)
    lane = lax.broadcasted_iota(jnp.int32, (places, LANES), 1)
    total = (total + SIDES - 1) // SIDES
    listed[...] = jnp.where(lane == LANES - 1, total, entries.astype(jnp.int32))
    copy = pltpu.make_async_copy(listed, steps, sem)
    copy.start()
    tops[...] = jnp.zeros_like(tops)
    copy.wait()

    flat = blocks.reshape(outer * block_rows, width)

    blank = jnp.zeros((PACK * query_tokens, width), jnp.bfloat16)

    def one_step(step):
        sides = []
        packed = []
        for side in range(SIDES):
            first = side * PACK
            sides.append(rows[steps[first, step] & (span - 1)])
            queries = jnp.concatenate(
                [
                    flat[pl.ds(pl.multiple_of((steps[k, step] >> bits) * 16, 16), query_tokens), :]
                    for k in range(first, first + PACK)
                ],
                axis=0,
            )
            packed.append(
                jnp.concatenate([queries if at == side else blank for at in range(SIDES)], axis=1)
            )
        dots = lax.dot_general(
            jnp.concatenate(sides, axis=1),
            jnp.concatenate(packed, axis=0),
            (((1,), (1,)), ((), ())),
            preferred_element_type=jnp.float32,
        )
        best = jnp.max(dots.reshape(2, slots, places * query_tokens), axis=1)
        tops[step : step + 1, :] = best[0:1]
        tops[max_steps + step : max_steps + step + 1, :] = best[1:2]

    taken = steps[0, LANES - 1]
    for begin, end in zip(CUTS, CUTS[1:] + (max_steps,)):

        @pl.when(taken > begin)
        def _():
            for step in range(begin, end):
                one_step(step)

    shape = (places, places * query_tokens)
    own = lax.broadcasted_iota(jnp.int32, shape, 1) // query_tokens
    own = (own == lax.broadcasted_iota(jnp.int32, shape, 0)).astype(jnp.float32)
    parts = lax.dot_general(
        own.astype(jnp.bfloat16),
        jnp.concatenate(pieces(tops[...]), axis=0),
        (((1,), (1,)), ((), ())),
        preferred_element_type=jnp.float32,
    )
    rows_of = 2 * max_steps
    sums = parts[:, :rows_of] + parts[:, rows_of : 2 * rows_of] + parts[:, 2 * rows_of :]
    by_step = in_step[:max_steps]
    spread = [
        exact_dot(sums[:, at * max_steps : (at + 1) * max_steps], by_step, ((1,), (0,)))
        for at in range(2)
    ]
    exact = jnp.sum(jnp.where(here, spread[0], 0.0), axis=0, keepdims=True)
    approx = jnp.sum(jnp.where(here, spread[1], 0.0), axis=0, keepdims=True)
    shape = (shards, 2 * pairs)
    pair = lax.broadcasted_iota(jnp.int32, shape, 1)
    from_shard = pair % pairs // cap == lax.broadcasted_iota(jnp.int32, shape, 0)
    scores = jnp.where(from_shard, jnp.concatenate([exact, approx], axis=1), 0.0)
    shape = (LANES, 2 * pairs)
    pair = lax.broadcasted_iota(jnp.int32, shape, 1)
    lane = pair // pairs * (LANES // 2) + pair % cap
    to_lane = (lax.broadcasted_iota(jnp.int32, shape, 0) == lane).astype(jnp.float32)
    back = exact_dot(scores, to_lane, ((1,), (1,)))
    for k, offset in enumerate(offsets):
        out[jnp.bitwise_xor(me, offset)] = back[k : k + 1, :]


def score(blocks, rows, offsets, query_tokens, cap, ways):
    passages, doubled, width = rows.shape
    shards = len(offsets)
    places = SIDES * PACK
    max_steps = -(-(shards * cap + (PACK - 1) * passages) // (8 * places)) * 8
    return pl.pallas_call(
        functools.partial(score_kernel, query_tokens, cap, ways, offsets),
        out_shape=pltpu.VMEM((shards, 1, LANES), jnp.float32),
        scratch_shapes=[
            pltpu.VMEM((places, LANES), jnp.int32),
            pltpu.SMEM((places, LANES), jnp.int32),
            pltpu.VMEM((2 * max_steps, places * query_tokens), jnp.float32),
            pltpu.SemaphoreType.DMA,
        ],
        compiler_params=pltpu.CompilerParams(vmem_limit_bytes=48 * 2**20),
        cost_estimate=pl.CostEstimate(
            flops=2 * max_steps * places * query_tokens * doubled * width,
            bytes_accessed=2 * (blocks.size + rows.size),
            transcendentals=0,
        ),
    )(blocks, rows)


def pick_kernel(plan, scores, exact_out, approx_out):
    q_local, top_k = exact_out.shape
    shards, padded, lanes = scores.shape
    slots = q_local * top_k
    target = plan[0:1, :]
    rank = plan[1:2, :]
    source = lax.broadcasted_iota(jnp.int32, (shards * padded, slots), 0)
    hot = (source == target * padded).astype(jnp.bfloat16)
    values = scores[...].reshape(shards * padded, lanes)
    spread = sum(
        lax.dot_general(
            part, hot, (((0,), (0,)), ((), ())), preferred_element_type=jnp.float32
        )
        for part in pieces(values)
    )
    lane = lax.broadcasted_iota(jnp.int32, (lanes, slots), 0)
    exact = jnp.sum(jnp.where(lane == rank, spread, 0.0), axis=0, keepdims=True)
    approx = jnp.sum(jnp.where(lane == rank + lanes // 2, spread, 0.0), axis=0, keepdims=True)
    for q in range(q_local):
        exact_out[q : q + 1, :] = exact[:, q * top_k : (q + 1) * top_k]
        approx_out[q : q + 1, :] = approx[:, q * top_k : (q + 1) * top_k]


def pick(plan, scores, shape):
    result = jax.ShapeDtypeStruct(shape, jnp.float32)
    operands = [pltpu.with_memory_space_constraint(x, pltpu.VMEM) for x in (plan, scores)]
    return pl.pallas_call(pick_kernel, out_shape=(result, result))(*operands)


def exchange(block, steps, shards):
    others = [
        lax.ppermute(block, "shard", [(i, i ^ step) for i in range(shards)]) for step in steps
    ]
    return [block] + others


def per_device(queries, centroids, codes, residual_codes, lengths, bucket_weights, candidates):
    shards = lax.axis_size("shard")
    passages = codes.shape[0]
    q_local, query_tokens, width = queries.shape
    tokens = q_local * query_tokens
    cap = max(2, 2 * candidates.size // shards)
    first_ways = 4 if shards % 4 == 0 else 2
    block, plan = make_plan(
        queries.reshape(tokens, width), candidates, shards, cap, passages, first_ways
    )
    block, codes = lax.optimization_barrier((block, codes))
    early = fetch(lengths, bucket_weights, codes, residual_codes, centroids, first_ways)
    offsets = [0]
    stride = shards
    while stride > 1:
        ways = 4 if stride % 4 == 0 else 2
        steps = [stride // ways * k for k in range(ways - 1, 0, -1)]
        blocks = exchange(block, steps, shards)
        if stride == shards:
            block = jnp.concatenate([x[:tokens] for x in blocks] + [sum(x[tokens:] for x in blocks)])
        else:
            block = jnp.concatenate(blocks)
        offsets = [k ^ at for k in [0] + steps for at in offsets]
        stride //= ways
        if stride > 1:
            block, lengths = lax.optimization_barrier((block, lengths))
    rows = decompress(
        lengths, bucket_weights, codes, residual_codes, centroids, first_ways, early
    )
    blocks = block.reshape(shards // first_ways, first_ways * tokens + META, width)
    scores = score(blocks, rows, offsets, query_tokens, cap, first_ways)
    back = lax.all_to_all(scores, "shard", split_axis=0, concat_axis=0, tiled=True)
    return pick(plan, back, candidates.shape)


def solution(mesh):
    placed = (
        P(("rep", "shard"), None, None),
        P("shard", None),
        P("shard", None),
        P("shard", None, None),
        P("shard"),
        P(),
        P(("rep", "shard"), None),
    )
    return jax.shard_map(
        per_device,
        mesh=mesh,
        in_specs=placed,
        out_specs=(P(("rep", "shard"), None), P(("rep", "shard"), None)),
        check_vma=False,
    )
```
